128 devices in a mesh: ctx: 64 (over y, z, x), srv: 2 (over core).
Axes of the slice: x: 4, y: 4, z: 4, core: 2. Of those that a mesh axis runs over, the one named last changes fastest.
Arguments:
- tokens: bfloat16 [16384, 2048], P('ctx'), may hold values from -6 to 6
- norm_gain: float32 [2048], replicated, may hold values from 0.5 to 2
- q_gain: float32 [128], replicated, may hold values from 0.7 to 16
- k_gain: float32 [128], replicated, may hold values from 0.7 to 16
- w_query: bfloat16 [2048, 2048], P(None, 'srv'), may hold values from -0.125 to 0.125
- w_key: bfloat16 [2048, 256], replicated, may hold values from -0.125 to 0.125
- w_value: bfloat16 [2048, 256], replicated, may hold values from -0.125 to 0.125
- w_out: bfloat16 [2048, 2048], P('srv'), may hold values from -0.125 to 0.125
- doc_lengths: int32 [4], replicated, may hold values from 1 to 10240, 16384 in all
- stretch_offsets: int32 [64], P('ctx'), may hold values from 0 to 24288, as said below
Outputs:
- attn_out: bfloat16 [16384, 2048], P(('ctx', 'srv'))
The draws below stay inside these ranges and needn't reach their ends.
Inputs may be any that keep to these rules, and one draw needn't show every extreme that they name: `doc_lengths`: the lengths sum to 16384; the longest is exactly 10240. `stretch_offsets`: offsets rise from block to block by 256 to 511; the first is below 256; the last is exactly (63) * 256 + 32 * 255.
All inputs are finite; a program needn't handle non-finite values.
Results may differ from the reference program's by a relative error of at most 0.013.
The reference program's roundings to bfloat16 on the way count: a program that leaves them out, or rounds other values in their place, can miss the bound.
Values may be sent and summed in bfloat16 or wider, within the bound.
A program may use at most 128 MiB of HBM per device.

```python
import math
import jax
import jax.numpy as jnp
import numpy as np
from jax import lax

D = 2048
HEAD_DIM = 128
QH = 16
KVH = 2
TOK_CTX = 256
DOCS = 4
TOKENS = 16384
MOST_LEN = 10240
N_CTX = 64


def gain_values(key, lowest, highest):
    uniform_draw = jax.random.uniform(key, (HEAD_DIM,), jnp.float32)
    return jnp.exp(jnp.log(lowest) + uniform_draw * (jnp.log(highest) - jnp.log(lowest)))


def draw_q_gain(key, part):
    folded = jax.random.fold_in(key, 17)
    return gain_values(folded, 0.7, 2.5)


def draw_k_gain(key, part):
    folded = jax.random.fold_in(key, 29)
    return gain_values(folded, 0.7, 2.5)


def draw_stretch_offsets(key, part):
    folded = jax.random.fold_in(key, 41)
    first_gaps = jax.random.randint(folded, (N_CTX // 2,), 0, TOK_CTX, dtype=jnp.int32)
    second_gaps = TOK_CTX - 1 - first_gaps
    gap_sizes = jnp.stack([first_gaps, second_gaps], axis=1).reshape(N_CTX)
    return (jnp.cumsum(gap_sizes).astype(jnp.int32) + jnp.arange(N_CTX, dtype=jnp.int32) * TOK_CTX).astype(jnp.int32)


def levels(stream_key, shape, split, least, largest):
    def one(dim, shards_of):
        heights = jax.random.uniform(jax.random.fold_in(jax.random.fold_in(stream_key, 6), dim), (shards_of,), jnp.float32, least / len(split), largest / len(split))
        return jnp.repeat(jnp.exp(heights), shape[dim] // shards_of).reshape((-1,) + (1,) * (len(shape) - dim - 1))

    factor_of = one(*split[0])
    for cut in split[1:]:
        factor_of = factor_of * one(*cut)
    return factor_of


def split_up(count, total, most, slope):
    portions = [(1 << 20) // math.isqrt(rank ** slope) + 1 for rank in range(2, count + 1)]
    spare, given = total - most - (count - 1), [1] * (count - 1)
    while spare > 0:
        candidates = [i for i in range(count - 1) if given[i] < most]
        mass, budget = sum([portions[i] for i in candidates]), spare
        for i in candidates:
            extra = min(most - given[i], max(1, budget * portions[i] // mass), spare)
            given[i] = given[i] + extra
            spare = spare - extra
    return np.array([most] + given)


def uneven(own_key, amount, total, most, slope):
    if amount == 2:
        one = jax.random.randint(own_key, (), max(1, total - most), min(most, total - 1) + 1)
        return jnp.stack([one, total - one])
    lengths = jnp.asarray(split_up(amount, total, most, slope), jnp.int32)
    twos = (amount - 1) // 2
    source_of, taker = lengths[1:1 + 2 * twos:2], lengths[2:2 + 2 * twos:2]
    room = jnp.minimum(source_of - 1, most - taker)
    shifted = jax.random.randint(jax.random.fold_in(own_key, 1), (twos,), 0, 1 << 20) % (room + 1)
    lengths = lengths.at[1:1 + 2 * twos:2].set(source_of - shifted).at[2:2 + 2 * twos:2].set(taker + shifted)
    return lengths[jax.random.permutation(jax.random.fold_in(own_key, 2), amount)]


def gaussian(rng, shape, deviation, limit, split=(), kind=jnp.bfloat16):
    drawn = jax.random.normal(rng, shape, jnp.float32) * deviation
    if len(split) > 0:
        drawn = levels(rng, shape, split, -0.22, 0.18) * drawn
    return jnp.clip(drawn, min=-limit, max=limit).astype(kind)


def setup_inputs(seed: int = 0) -> dict:
    keys = jax.random.split(jax.random.key(seed), 11)
    tokens = gaussian(keys[0], (TOKENS, D), 1.0, 6.0, ((0, 64),))
    norm_gain = jnp.clip(jnp.exp(jax.random.uniform(keys[1], (D,), jnp.float32, math.log(0.5), math.log(2.0))), 0.5, 2.0)
    q_gain = draw_q_gain(jax.random.fold_in(keys[10], 71), 0)
    k_gain = draw_k_gain(jax.random.fold_in(keys[10], 71), 0)
    w_query = gaussian(keys[4], (D, QH * HEAD_DIM), D ** -0.5, 0.125, ((1, 2),))
    w_key = gaussian(keys[5], (D, KVH * HEAD_DIM), D ** -0.5, 0.125)
    w_value = gaussian(keys[6], (D, KVH * HEAD_DIM), D ** -0.5, 0.125)
    w_out = gaussian(keys[7], (QH * HEAD_DIM, D), (QH * HEAD_DIM) ** -0.5, 0.125, ((0, 2),))
    doc_lengths = uneven(keys[8], DOCS, TOKENS, MOST_LEN, 2).astype(jnp.int32)
    stretch_offsets = draw_stretch_offsets(jax.random.fold_in(keys[10], 71), 0)
    return {"tokens": tokens, "norm_gain": norm_gain, "q_gain": q_gain, "k_gain": k_gain, "w_query": w_query, "w_key": w_key, "w_value": w_value, "w_out": w_out, "doc_lengths": doc_lengths, "stretch_offsets": stretch_offsets}


rope_base = 1000000.0
norm_eps = 1e-06
masked_score = -1e+30

def rms_scale(values, weights):
    mean_square = lax.optimization_barrier(jnp.mean(values * values, axis=-1, keepdims=True))
    return values * lax.rsqrt(mean_square + norm_eps) * weights

def rotate(values, positions):
    half_dim = values.shape[-1] // 2
    frequency = rope_base ** (-2.0 * jnp.arange(half_dim, dtype=jnp.float32) / values.shape[-1])
    angles = positions.astype(jnp.float32)[:, None] * frequency[None, :]
    cosine = jnp.cos(angles)[:, None, :]
    sine_part = jnp.sin(angles)[:, None, :]
    first_half = values[..., :half_dim]
    second_half = values[..., half_dim:]
    return jnp.concatenate([first_half * cosine - second_half * sine_part, second_half * cosine + first_half * sine_part], axis=-1)

def segment_of(indices, doc_ends):
    return lax.optimization_barrier(jnp.sum((indices[None, :] >= doc_ends[:, None]).astype(jnp.int32), axis=0))

def reference(tokens, norm_gain, q_gain, k_gain, w_query, w_key, w_value, w_out, doc_lengths, stretch_offsets):
    total_rows = tokens.shape[0]
    group_size = QH // KVH
    score_scale = HEAD_DIM ** (-0.5)
    normed = rms_scale(tokens.astype(jnp.float32), norm_gain).astype(jnp.bfloat16)
    all_index = jnp.arange(total_rows, dtype=jnp.int32)
    positions = (stretch_offsets[all_index // TOK_CTX] + all_index % TOK_CTX).astype(jnp.int32)
    doc_ends = jnp.cumsum(doc_lengths).astype(jnp.int32)
    segments = segment_of(all_index, doc_ends)
    queries = jnp.dot(normed, w_query, preferred_element_type=jnp.float32).reshape(total_rows, QH, HEAD_DIM)
    queries = rotate(rms_scale(queries, q_gain), positions).astype(jnp.bfloat16)
    queries = lax.optimization_barrier(queries).reshape(total_rows, KVH, group_size, HEAD_DIM)
    keys_all = jnp.dot(normed, w_key, preferred_element_type=jnp.float32).reshape(total_rows, KVH, HEAD_DIM)
    keys_all = rotate(rms_scale(keys_all, k_gain), positions).astype(jnp.bfloat16)
    keys_wide = lax.optimization_barrier(keys_all).astype(jnp.float32)
    values_all = jnp.dot(normed, w_value, preferred_element_type=jnp.float32).astype(jnp.bfloat16)
    values_all = lax.optimization_barrier(values_all).astype(jnp.float32).reshape(total_rows, KVH, HEAD_DIM)
    block_rows = math.gcd(total_rows, 512)

    def attend(block_start):
        query_block = lax.dynamic_slice_in_dim(queries, block_start, block_rows, 0).astype(jnp.float32)
        query_index = block_start + jnp.arange(block_rows, dtype=jnp.int32)
        query_segment = lax.dynamic_slice_in_dim(segments, block_start, block_rows, 0)
        allowed = (query_segment[:, None] == segments[None, :]) & (all_index[None, :] <= query_index[:, None])
        scores = jnp.einsum('tkgd,pkd->kgtp', query_block, keys_wide) * score_scale
        scores = jnp.where(allowed[None, None], scores, masked_score)
        top_score = lax.optimization_barrier(jnp.max(scores, axis=-1, keepdims=True))
        exponent = jnp.where(allowed[None, None], jnp.exp(scores - top_score), 0.0)
        denominator = lax.optimization_barrier(jnp.sum(exponent, axis=-1))
        weights = lax.optimization_barrier(exponent.astype(jnp.bfloat16)).astype(jnp.float32)
        mixed_heads = jnp.einsum('kgtp,pkd->kgtd', weights, values_all) / denominator[..., None]
        return jnp.transpose(mixed_heads, (2, 0, 1, 3)).reshape(block_rows, QH * HEAD_DIM)
    starts = jnp.arange(total_rows // block_rows, dtype=jnp.int32) * block_rows
    attended = lax.map(attend, starts).reshape(total_rows, QH * HEAD_DIM).astype(jnp.bfloat16)
    return jnp.dot(attended, w_out, preferred_element_type=jnp.float32).astype(jnp.bfloat16)
```

```python
import math

import jax
import jax.numpy as jnp
import numpy as np
from jax import lax
from jax.experimental import pallas as pl
from jax.experimental.pallas import tpu as pltpu
from jax.sharding import PartitionSpec as P

rope_base = 1000000.0
norm_eps = 1e-06
masked_score = -1e30
HEAD = 128
ROWS = 256
BLOCKS = 64
REACH = 40
MESH = pl.DeviceIdType.MESH
F32 = jnp.float32
BF16 = jnp.bfloat16

hop_table = (
    (16, 48, 4, 12, 1, 3),
    (32, 49, 8, 28, 17, 19),
    (35, 56, 21, 44, 5, 7),
    (20, 51, 11, 31, 13, 34),
    (23, 40, 38, 61, 45, 15),
    (33, 53, 55, 29, 57, 30),
    (27, 59, 42, 26, 62, 18),
    (0, 52, 39, 25, 9, 54),
    (0, 36, 22, 24, 41, 10),
    (0, 37, 0, 60, 6, 47),
    (0, 63, 0, 0, 14, 43),
    (0, 0, 0, 0, 46, 58),
    (0, 0, 0, 0, 50, 0),
    (0, 0, 0, 0, 2, 0),
)

ways = ((1, 0, 0), (3, 0, 0), (0, 1, 0), (0, 3, 0), (0, 0, 1), (0, 0, 3))


def apart(index):
    return (index // 16, index // 4 % 4, index % 4)


def joined(a, b, sign=1):
    y, z, x = ((p + sign * q) % 4 for p, q in zip(a, b))
    return y * 16 + z * 4 + x


SLOTS = len(hop_table)
STRIDE = 4


def plan():
    hops = {d: (s, w) for s, row in enumerate(hop_table) for w, d in enumerate(row) if d}
    carried = {
        at: [0 <= c - joined(apart(c), apart(d), -1) <= REACH for c in range(BLOCKS)] for d, at in hops.items()
    }
    for d, (s, w) in sorted(hops.items(), key=lambda hop: -hop[1][0]):
        parent = joined(apart(d), ways[w], -1)
        if parent:
            for c in range(BLOCKS):
                if carried[s, w][joined(apart(c), ways[w])]:
                    carried[hops[parent]][c] = True
    return carried


carried_at = plan()


def looked_up(i):
    flat = [d for row in hop_table for d in row]
    words = [sum(d << 6 * k for k, d in enumerate(flat[at : at + 5])) for at in range(0, len(flat), 5)]
    word, group = jnp.int32(words[0]), i // 5
    for k in range(1, len(words)):
        word = jnp.where(group == k, jnp.int32(words[k]), word)
    return lax.shift_right_logical(word, 6 * lax.rem(i, 5)) & 63


def spans(row):
    out, start = [], None
    for c in range(BLOCKS + 1):
        inside = c < BLOCKS and row[c]
        if inside and start is None:
            start = c
        if not inside and start is not None:
            out.append((start, c - 1))
            start = None
    return out


def among(row, chip):
    found = None
    for first, last in spans(row):
        one = (chip >= first) & (chip <= last)
        found = one if found is None else found | one
    return chip < 0 if found is None else found


def sine_cosine(angle):
    turns = jnp.floor(angle * (2.0 / math.pi) + 0.5)
    rest = angle
    for part in quarter_parts:
        rest = rest - turns * part
    square = rest * rest
    s = rest + rest * square * (
        -1.6666666666e-1 + square * (8.3333331876e-3 + square * (-1.9841270114e-4 + square * 2.7557314e-6))
    )
    c = 1.0 + square * (
        -0.5 + square * (4.16666666e-2 + square * (-1.3888888e-3 + square * (2.4801587e-5 - square * 2.7557e-7)))
    )
    quarter = turns.astype(jnp.int32) & 3
    odd = (quarter & 1) == 1
    sine, cosine = jnp.where(odd, c, s), jnp.where(odd, s, c)
    sine = jnp.where(quarter >= 2, -sine, sine)
    cosine = jnp.where((quarter == 1) | (quarter == 2), -cosine, cosine)
    return sine, cosine


def split_quarter():
    parts, left = [], math.pi / 2
    for _ in range(3):
        exponent = math.floor(math.log2(left))
        unit = 2.0 ** (exponent - 7)
        part = math.floor(left / unit) * unit
        parts.append(part)
        left -= part
    return (*parts, left)


quarter_parts = split_quarter()
score_scale_2 = math.log2(math.e) * HEAD ** (-0.5)


def scaled_and_rotated(x, gain, sine, cosine):
    x = x * lax.rsqrt(jnp.mean(x * x, axis=0, keepdims=True) + norm_eps) * gain
    a, b = x[:64], x[64:]
    return jnp.concatenate([a * cosine - b * sine, b * cosine + a * sine], axis=0)


def column(row_vector):
    square = jnp.broadcast_to(row_vector, (HEAD, HEAD)).T
    return jnp.concatenate([square, square], axis=1)


def kernel(
    tokens, norm_gain, q_gain, k_gain, frequency, w_query, w_key, w_value, w_out, doc_lengths, offsets,
    out, x_buf, normed, wkv, wq, wo, kv, q_t, score, weight, state, top, attended, sent, received,
    load_sem, q_sem, send_sem, recv_sem, swap_sem,
):
    chip, server = lax.axis_index("ctx"), lax.axis_index("srv")
    cy, cz, cx = chip // 16, lax.rem(chip // 4, 4), lax.rem(chip, 4)

    def moved(step, sign=1):
        dy, dz, dx = step
        if sign < 0:
            dy, dz, dx = (4 - dy) % 4, (4 - dz) % 4, (4 - dx) % 4
        return lax.rem(cy + dy, 4) * 16 + lax.rem(cz + dz, 4) * 4 + lax.rem(cx + dx, 4)

    neighbours = [moved(w) for w in ways]
    barrier = pltpu.get_barrier_semaphore()
    for n in neighbours:
        pl.semaphore_signal(barrier, inc=1, device_id={"ctx": n}, device_id_type=MESH)
    pl.semaphore_signal(barrier, inc=1, device_id={"srv": 1 - server}, device_id_type=MESH)

    lanes = pl.ds(pl.multiple_of(server * HEAD, HEAD), HEAD)
    load_x = pltpu.make_async_copy(tokens, x_buf, load_sem.at[0])
    load_k = pltpu.make_async_copy(w_key.at[:, lanes], wkv.at[:, :HEAD], load_sem.at[1])
    load_v = pltpu.make_async_copy(w_value.at[:, lanes], wkv.at[:, HEAD:], load_sem.at[2])
    load_o = pltpu.make_async_copy(w_out, wo, load_sem.at[3])
    load_q = [
        pltpu.make_async_copy(w_query.at[:, i * 256 : (i + 1) * 256], wq.at[i], q_sem.at[i]) for i in range(4)
    ]
    for copy in (load_x, load_k, load_v, *load_q, load_o):
        copy.start()

    offset = offsets[0]
    token_lane = lax.broadcasted_iota(jnp.int32, (8, ROWS), 1)
    position = (token_lane + offset).astype(F32)[:1]
    sine, cosine = sine_cosine(
        jnp.concatenate([frequency[...], frequency[...]], axis=1) * jnp.broadcast_to(position, (64, ROWS))
    )
    lengths = [doc_lengths[i] for i in range(4)]
    ends = [lengths[0]]
    for i in range(1, 4):
        ends.append(ends[-1] + lengths[i])
    starts = [jnp.int32(0), *ends[:3]]
    feature = lax.broadcasted_iota(jnp.int32, (1, HEAD), 1)
    first_of = jnp.full((1, HEAD), 1 << 30, jnp.int32)
    end_of = jnp.full((1, HEAD), 1 << 30, jnp.int32)
    for i in range(4):
        first_of = jnp.where(feature == i, starts[i], first_of)
        end_of = jnp.where(feature == i, ends[i], end_of)
    feature_row = lax.broadcasted_iota(jnp.int32, (HEAD, ROWS), 0)
    token = lax.broadcasted_iota(jnp.int32, (HEAD, ROWS), 1) + chip * ROWS
    barred = jnp.zeros((HEAD, ROWS), F32)
    for i in range(4):
        outside = (token < starts[i]) | (token >= ends[i])
        barred = jnp.where((feature_row == i) & outside, masked_score, barred)
    barred = barred.astype(BF16)
    for h in range(8):
        q_t[HEAD:, h * ROWS : (h + 1) * ROWS] = barred

    load_x.wait()

    def norm_rows(i, carry):
        at = pl.ds(pl.multiple_of(i * 32, 32), 32)
        x = x_buf[at, :].astype(F32)
        x = x * lax.rsqrt(jnp.mean(x * x, axis=1, keepdims=True) + norm_eps) * norm_gain[...]
        normed[at, :] = x.astype(BF16)
        return carry

    lax.fori_loop(0, 8, norm_rows, 0)

    load_k.wait()
    load_v.wait()
    pair = jnp.dot(normed[...], wkv[...], preferred_element_type=F32)
    key = scaled_and_rotated(pair[:, :HEAD].T, column(k_gain[...]), sine, cosine).T.astype(BF16)
    value = pair[:, HEAD:].T.astype(BF16)
    kv[chip, :, :HEAD] = key
    kv[chip, :HEAD, HEAD:] = value[:, :HEAD]
    kv[chip, HEAD:, HEAD:] = value[:, HEAD:]

    def gathered(w, at):
        bits = jnp.int32(0)
        for t in range(SLOTS):
            if (t, w) in carried_at:
                bits += jnp.where(among(carried_at[t, w], at), 1 << t, 0)
        return bits

    takes = [gathered(w, chip) for w in range(6)]
    gives = [gathered(w, neighbours[w]) for w in range(6)]

    def set_in(bits, t):
        return lax.rem(lax.shift_right_logical(bits, t), 2) == 1

    def behind(y, z, x):
        return lax.rem(y + 4, 4) * 16 + lax.rem(z + 4, 4) * 4 + lax.rem(x + 4, 4)

    def hop(t, w, block):
        at = t * 6 + w
        return pltpu.make_async_remote_copy(
            src_ref=kv.at[block],
            dst_ref=kv.at[block],
            send_sem=send_sem.at[at],
            recv_sem=recv_sem.at[at],
            device_id={"ctx": neighbours[w]},
            device_id_type=MESH,
        )

    def hand_on(t):
        for w in range(6):

            @pl.when(set_in(gives[w], t))
            def _():
                d, (uy, uz, ux) = looked_up(t * 6 + w), ways[w]
                block = behind(cy - d // 16 + uy % 3 - uy // 3, cz - lax.rem(d // 4, 4) + uz % 3 - uz // 3, cx - lax.rem(d, 4) + ux % 3 - ux // 3)
                hop(t, w, block).start()

    def arrive(t):
        for w in range(6):

            @pl.when(set_in(takes[w], t))
            def _():
                d = looked_up(t * 6 + w)
                hop(t, w, behind(cy - d // 16, cz - lax.rem(d // 4, 4), cx - lax.rem(d, 4))).wait_recv()

    pl.semaphore_wait(barrier, 7)
    hand_on(0)

    q_column = column(q_gain[...])
    for i in range(4):
        load_q[i].wait()
        two = jnp.dot(normed[...], wq[i], preferred_element_type=F32)
        for u in range(2):
            h = 2 * i + u
            x = scaled_and_rotated(two[:, u * HEAD : (u + 1) * HEAD].T, q_column, sine, cosine)
            q_t[:HEAD, h * ROWS : (h + 1) * ROWS] = x.astype(BF16)

    ones = jnp.ones((16, ROWS), BF16)

    def attend(block, own):
        key_at = lax.broadcasted_iota(jnp.int32, (ROWS, HEAD), 0) + block * ROWS
        segment = jnp.where((key_at >= first_of) & (key_at < end_of), 1.0, 0.0).astype(BF16)
        keys = jnp.concatenate([kv[block, :, :HEAD], segment], axis=1)
        values = jnp.concatenate([kv[block, :HEAD, HEAD:], kv[block, HEAD:, HEAD:]], axis=1)
        values = jnp.concatenate([values, ones], axis=0)
        for h in range(8):
            at = slice(h * ROWS, (h + 1) * ROWS)
            s = jnp.dot(keys, q_t[:, at], preferred_element_type=F32)
            if own:
                later = lax.broadcasted_iota(jnp.int32, s.shape, 0) > lax.broadcasted_iota(jnp.int32, s.shape, 1)
                s = jnp.where(later, masked_score, s)
            score[:, at] = s
        for h in range(8):
            at = slice(h * ROWS, (h + 1) * ROWS)
            s = score[:, at]
            highest = jnp.max(s, axis=0, keepdims=True) * score_scale_2
            if not own:
                before = top[:, at]
                highest = jnp.maximum(before, highest)
                state[:, at] = state[:, at] * jnp.exp2(before - highest)[:1]
            else:
                highest = jnp.broadcast_to(highest, (8, ROWS))
            top[:, at] = highest
            weight[:, at] = jnp.exp2(s * score_scale_2 - highest[:1]).astype(BF16)
        for h in range(8):
            at = slice(h * ROWS, (h + 1) * ROWS)
            mixed = jnp.dot(values, weight[:, at], preferred_element_type=F32)
            if own:
                state[:, at] = mixed
            else:
                state[:, at] += mixed

    attend(chip, True)

    def compute(i, carry):
        d = looked_up(i)
        block = behind(cy - d // 16, cz - lax.rem(d // 4, 4), cx - lax.rem(d, 4))

        @pl.when((block < chip) & (block >= chip - REACH))
        def _():
            attend(block, False)

        return carry

    def slot(t, carry):
        arrive(t - 1)

        @pl.when(t < SLOTS)
        def _():
            hand_on(t)

        first = (t - 1) * STRIDE
        lax.fori_loop(first, jnp.where(t < SLOTS, first + STRIDE, SLOTS * 6), compute, 0)
        return carry

    lax.fori_loop(1, SLOTS + 1, slot, 0)

    load_o.wait()
    for h in range(8):
        at = slice(h * ROWS, (h + 1) * ROWS)
        x = state[:HEAD, at] * (1.0 / state[HEAD : HEAD + 1, at])
        attended[:, h * HEAD : (h + 1) * HEAD] = x.T.astype(BF16)
    theirs = pl.ds(pl.multiple_of((1 - server) * HEAD, HEAD), HEAD)
    mine = pl.ds(pl.multiple_of(server * HEAD, HEAD), HEAD)
    swaps = []
    for n in range(4):
        at = slice(n * 512, (n + 1) * 512)
        sent[n] = jnp.dot(attended[theirs, :], wo[:, at], preferred_element_type=F32).astype(BF16)
        swap = pltpu.make_async_remote_copy(
            src_ref=sent.at[n],
            dst_ref=received.at[n],
            send_sem=swap_sem.at[0, n],
            recv_sem=swap_sem.at[1, n],
            device_id={"srv": 1 - server},
            device_id_type=MESH,
        )
        swap.start()
        swaps.append(swap)
    for n in range(4):
        at = slice(n * 512, (n + 1) * 512)
        part = jnp.dot(attended[mine, :], wo[:, at], preferred_element_type=F32)
        swaps[n].wait_recv()
        out[:, at] = (part + received[n].astype(F32)).astype(BF16)
    for n in range(4):
        swaps[n].wait_send()

    def left(t, carry):
        for w in range(6):

            @pl.when(set_in(gives[w], t))
            def _():
                hop(t, w, chip).wait_send()

        return carry

    lax.fori_loop(0, SLOTS, left, 0)


def local(
    tokens, norm_gain, q_gain, k_gain, w_query, w_key, w_value, w_out, doc_lengths, stretch_offsets
):
    frequency = rope_base ** (-2.0 * jnp.arange(HEAD // 2, dtype=F32) / HEAD)
    frequency = jnp.broadcast_to(frequency[:, None], (HEAD // 2, HEAD))
    vmem = pl.BlockSpec(memory_space=pltpu.VMEM)
    smem = pl.BlockSpec(memory_space=pltpu.SMEM)
    hbm = pl.BlockSpec(memory_space=pl.ANY)
    dma = pltpu.SemaphoreType.DMA
    return pl.pallas_call(
        kernel,
        out_shape=jax.ShapeDtypeStruct((HEAD, 2048), BF16),
        in_specs=[hbm, vmem, vmem, vmem, vmem, hbm, hbm, hbm, hbm, smem, smem],
        out_specs=vmem,
        scratch_shapes=[
            pltpu.VMEM((ROWS, 2048), BF16),
            pltpu.VMEM((ROWS, 2048), BF16),
            pltpu.VMEM((2048, 256), BF16),
            pltpu.VMEM((4, 2048, 256), BF16),
            pltpu.VMEM((1024, 2048), BF16),
            pltpu.VMEM((BLOCKS, ROWS, 256), BF16),
            pltpu.VMEM((256, 2048), BF16),
            pltpu.VMEM((ROWS, 2048), F32),
            pltpu.VMEM((ROWS, 2048), BF16),
            pltpu.VMEM((HEAD + 16, 2048), F32),
            pltpu.VMEM((8, 2048), F32),
            pltpu.VMEM((ROWS, 1024), BF16),
            pltpu.VMEM((4, HEAD, 512), BF16),
            pltpu.VMEM((4, HEAD, 512), BF16),
            dma((4,)),
            dma((4,)),
            dma((SLOTS * 6,)),
            dma((SLOTS * 6,)),
            dma((2, 4)),
        ],
        compiler_params=pltpu.CompilerParams(
            collective_id=0, has_side_effects=True, vmem_limit_bytes=60 * 2**20
        ),
        name="attention_layer",
    )(
        tokens,
        norm_gain.reshape(1, -1),
        q_gain.reshape(1, -1),
        k_gain.reshape(1, -1),
        frequency,
        w_query,
        w_key,
        w_value,
        w_out,
        doc_lengths,
        stretch_offsets,
    )


def solution(mesh):
    return jax.shard_map(
        local,
        mesh=mesh,
        in_specs=(
            P("ctx", None),
            P(),
            P(),
            P(),
            P(None, "srv"),
            P(),
            P(),
            P("srv", None),
            P(),
            P("ctx"),
        ),
        out_specs=P(("ctx", "srv"), None),
        check_vma=False,
    )
```

```python
import math

import jax
import jax.numpy as jnp
import numpy as np
from jax import lax
from jax.experimental import pallas as pl
from jax.experimental.pallas import tpu as pltpu
from jax.sharding import PartitionSpec as P

rope_base = 1000000.0
norm_eps = 1e-06
masked_score = -1e30
HEAD = 128
ROWS = 256
BLOCKS = 64
REACH = 40
WIDE = 2048
MESH = pl.DeviceIdType.MESH
F32 = jnp.float32
BF16 = jnp.bfloat16

hop_table = (
    (16, 48, 4, 12, 1, 3),
    (0, 0, 0, 0, 0, 0),
    (17, 52, 8, 28, 5, 7),
    (0, 32, 20, 60, 49, 19),
    (21, 53, 11, 29, 6, 55),
    (35, 36, 56, 31, 9, 2),
    (27, 37, 59, 24, 18, 10),
    (47, 57, 39, 25, 61, 34),
    (23, 54, 41, 30, 22, 15),
    (43, 50, 38, 46, 26, 0),
    (45, 63, 58, 13, 62, 14),
    (40, 51, 0, 44, 33, 42),
)

ways = ((1, 0, 0), (3, 0, 0), (0, 1, 0), (0, 3, 0), (0, 0, 1), (0, 0, 3))


def apart(index):
    return (index // 16, index // 4 % 4, index % 4)


def joined(a, b, sign=1):
    y, z, x = ((p + sign * q) % 4 for p, q in zip(a, b))
    return y * 16 + z * 4 + x


SLOTS = len(hop_table)
LAG = 2


def plan():
    hops = {d: (s, w) for s, row in enumerate(hop_table) for w, d in enumerate(row) if d}
    carried = {
        at: [0 <= c - joined(apart(c), apart(d), -1) <= REACH for c in range(BLOCKS)] for d, at in hops.items()
    }
    for d, (s, w) in sorted(hops.items(), key=lambda hop: -hop[1][0]):
        parent = joined(apart(d), ways[w], -1)
        if parent:
            for c in range(BLOCKS):
                if carried[s, w][joined(apart(c), ways[w])]:
                    carried[hops[parent]][c] = True
    return carried


carried_at = plan()


def looked_up(i):
    flat = [d for row in hop_table for d in row]
    words = [sum(d << 6 * k for k, d in enumerate(flat[at : at + 5])) for at in range(0, len(flat), 5)]
    word, group = jnp.int32(words[0]), i // 5
    for k in range(1, len(words)):
        word = jnp.where(group == k, jnp.int32(words[k]), word)
    return lax.shift_right_logical(word, 6 * lax.rem(i, 5)) & 63


def spans(row):
    out, start = [], None
    for c in range(BLOCKS + 1):
        inside = c < BLOCKS and row[c]
        if inside and start is None:
            start = c
        if not inside and start is not None:
            out.append((start, c - 1))
            start = None
    return out


def among(row, chip):
    found = None
    for first, last in spans(row):
        one = (chip >= first) & (chip <= last)
        found = one if found is None else found | one
    return chip < 0 if found is None else found


def sine_cosine(angle):
    turns = jnp.floor(angle * (2.0 / math.pi) + 0.5)
    rest = angle
    for part in quarter_parts:
        rest = rest - turns * part
    square = rest * rest
    s = rest + rest * square * (
        -1.6666666666e-1 + square * (8.3333331876e-3 + square * (-1.9841270114e-4 + square * 2.7557314e-6))
    )
    c = 1.0 + square * (
        -0.5 + square * (4.16666666e-2 + square * (-1.3888888e-3 + square * (2.4801587e-5 - square * 2.7557e-7)))
    )
    quarter = turns.astype(jnp.int32) & 3
    odd = (quarter & 1) == 1
    sine, cosine = jnp.where(odd, c, s), jnp.where(odd, s, c)
    sine = jnp.where(quarter >= 2, -sine, sine)
    cosine = jnp.where((quarter == 1) | (quarter == 2), -cosine, cosine)
    return sine, cosine


def split_quarter():
    parts, left = [], math.pi / 2
    for _ in range(3):
        exponent = math.floor(math.log2(left))
        unit = 2.0 ** (exponent - 7)
        part = math.floor(left / unit) * unit
        parts.append(part)
        left -= part
    return (*parts, left)


quarter_parts = split_quarter()
score_scale_2 = math.log2(math.e) * HEAD ** (-0.5)


def scaled_and_rotated(x, gain, sine, cosine):
    x = x * lax.rsqrt(jnp.mean(x * x, axis=0, keepdims=True) + norm_eps) * gain
    a, b = x[:64], x[64:]
    return jnp.concatenate([a * cosine - b * sine, b * cosine + a * sine], axis=0)


def column(row_vector):
    square = jnp.broadcast_to(row_vector, (HEAD, HEAD)).T
    return jnp.concatenate([square, square], axis=1)


def kernel(
    tokens, norm_gain, q_gain, k_gain, frequency, w_query, w_key, w_value, w_out, doc_lengths, offsets,
    out, x_buf, normed, wkv, wq, wo, kv, q_t, score, peak, weight, factor, state, top, attended, sent, received,
    load_sem, q_sem, send_sem, recv_sem, swap_sem,
):
    chip, server = lax.axis_index("ctx"), lax.axis_index("srv")
    cy, cz, cx = chip // 16, lax.rem(chip // 4, 4), lax.rem(chip, 4)

    def moved(step, sign=1):
        dy, dz, dx = step
        if sign < 0:
            dy, dz, dx = (4 - dy) % 4, (4 - dz) % 4, (4 - dx) % 4
        return lax.rem(cy + dy, 4) * 16 + lax.rem(cz + dz, 4) * 4 + lax.rem(cx + dx, 4)

    neighbours = [moved(w) for w in ways]
    barrier = pltpu.get_barrier_semaphore()
    for n in neighbours:
        pl.semaphore_signal(barrier, inc=1, device_id={"ctx": n}, device_id_type=MESH)
    pl.semaphore_signal(barrier, inc=1, device_id={"srv": 1 - server}, device_id_type=MESH)

    lanes = pl.ds(pl.multiple_of(server * HEAD, HEAD), HEAD)
    load_x = pltpu.make_async_copy(tokens, x_buf, load_sem.at[0])
    load_k = pltpu.make_async_copy(w_key.at[:, lanes], wkv.at[:, :HEAD], load_sem.at[1])
    load_v = pltpu.make_async_copy(w_value.at[:, lanes], wkv.at[:, HEAD:], load_sem.at[2])
    load_o = pltpu.make_async_copy(w_out, wo, load_sem.at[3])
    load_q = [
        pltpu.make_async_copy(w_query.at[:, i * 256 : (i + 1) * 256], wq.at[i], q_sem.at[i]) for i in range(4)
    ]
    for copy in (load_x, load_k, load_v, *load_q, load_o):
        copy.start()

    offset = offsets[0]
    token_lane = lax.broadcasted_iota(jnp.int32, (8, ROWS), 1)
    position = (token_lane + offset).astype(F32)[:1]
    sine, cosine = sine_cosine(column(frequency[...])[:64] * jnp.broadcast_to(position, (64, ROWS)))
    lengths = [doc_lengths[i] for i in range(4)]
    ends = [lengths[0]]
    for i in range(1, 4):
        ends.append(ends[-1] + lengths[i])
    starts = [jnp.int32(0), *ends[:3]]
    feature = lax.broadcasted_iota(jnp.int32, (1, HEAD), 1)
    first_of = jnp.full((1, HEAD), 1 << 30, jnp.int32)
    end_of = jnp.full((1, HEAD), 1 << 30, jnp.int32)
    for i in range(4):
        first_of = jnp.where(feature == i, starts[i], first_of)
        end_of = jnp.where(feature == i, ends[i], end_of)
    feature_row = lax.broadcasted_iota(jnp.int32, (HEAD, ROWS), 0)
    token = lax.broadcasted_iota(jnp.int32, (HEAD, ROWS), 1) + chip * ROWS
    barred = jnp.zeros((HEAD, ROWS), F32)
    for i in range(4):
        outside = (token < starts[i]) | (token >= ends[i])
        barred = jnp.where((feature_row == i) & outside, masked_score, barred)
    barred = barred.astype(BF16)
    for h in range(8):
        q_t[HEAD:, h * ROWS : (h + 1) * ROWS] = barred

    load_x.wait()

    def norm_rows(i, carry):
        at = pl.ds(pl.multiple_of(i * 32, 32), 32)
        x = x_buf[at, :].astype(F32)
        x = x * lax.rsqrt(jnp.mean(x * x, axis=1, keepdims=True) + norm_eps) * norm_gain[...]
        normed[at, :] = x.astype(BF16)
        return carry

    lax.fori_loop(0, 8, norm_rows, 0)

    load_k.wait()
    load_v.wait()
    pair = jnp.dot(normed[...], wkv[...], preferred_element_type=F32)
    key = scaled_and_rotated(pair[:, :HEAD].T, column(k_gain[...]), sine, cosine).T.astype(BF16)
    value = pair[:, HEAD:].T.astype(BF16)
    kv[chip, :, :HEAD] = key
    kv[chip, :HEAD, HEAD:] = value[:, :HEAD]
    kv[chip, HEAD:, HEAD:] = value[:, HEAD:]

    def gathered(w, at):
        bits = jnp.int32(0)
        for t in range(SLOTS):
            if (t, w) in carried_at:
                bits += jnp.where(among(carried_at[t, w], at), 1 << t, 0)
        return bits

    takes = [gathered(w, chip) for w in range(6)]
    gives = [gathered(w, neighbours[w]) for w in range(6)]

    def set_in(bits, t):
        return lax.rem(lax.shift_right_logical(bits, t), 2) == 1

    def behind(y, z, x):
        return lax.rem(y + 4, 4) * 16 + lax.rem(z + 4, 4) * 4 + lax.rem(x + 4, 4)

    def hop(t, w, block):
        return pltpu.make_async_remote_copy(
            src_ref=kv.at[block],
            dst_ref=kv.at[block],
            send_sem=send_sem.at[t * 6 + w],
            recv_sem=recv_sem.at[t * 6 + w],
            device_id={"ctx": neighbours[w]},
            device_id_type=MESH,
        )

    def block_at(d, way=(0, 0, 0)):
        uy, uz, ux = (u - 4 * (u == 3) for u in way)
        return behind(cy - d // 16 + uy, cz - lax.rem(d // 4, 4) + uz, cx - lax.rem(d, 4) + ux)

    pl.semaphore_wait(barrier, 7)
    for w in range(6):

        @pl.when(set_in(gives[w], 0))
        def _():
            hop(0, w, chip).start()


    q_column = column(q_gain[...])
    for i in range(4):
        load_q[i].wait()
        two = jnp.dot(normed[...], wq[i], preferred_element_type=F32)
        for u in range(2):
            h = 2 * i + u
            x = scaled_and_rotated(two[:, u * HEAD : (u + 1) * HEAD].T, q_column, sine, cosine)
            q_t[:HEAD, h * ROWS : (h + 1) * ROWS] = x.astype(BF16)

    ones = jnp.ones((16, ROWS), BF16)

    def scores(block, turn, own=False):
        key_at = lax.broadcasted_iota(jnp.int32, (ROWS, HEAD), 0) + block * ROWS
        segment = jnp.where((key_at >= first_of) & (key_at < end_of), 1.0, 0.0).astype(BF16)
        keys = jnp.concatenate([kv[block, :, :HEAD], segment], axis=1)
        step = ROWS if own else WIDE
        for at in range(0, 2048, step):
            at = slice(at, at + step)
            s = jnp.dot(keys, q_t[:, at], preferred_element_type=F32)
            if own:
                later = lax.broadcasted_iota(jnp.int32, s.shape, 0) > lax.broadcasted_iota(jnp.int32, s.shape, 1)
                s = jnp.where(later, masked_score, s)
            score[turn, :, at] = s
            peak[turn, :, at] = jnp.max(s.reshape(ROWS // 8, 8, step), axis=0)

    def softmax(turn):
        for at in range(0, 2048, WIDE):
            at = slice(at, at + WIDE)
            before = top[:, at]
            highest = jnp.maximum(before, jnp.max(peak[turn, :, at], axis=0, keepdims=True) * score_scale_2)
            top[:, at] = highest
            factor[turn, :, at] = jnp.exp2(before - highest)
            weight[turn, :, at] = jnp.exp2(score[turn, :, at] * score_scale_2 - highest[:1]).astype(BF16)

    def mix(block, turn):
        values = jnp.concatenate([kv[block, :HEAD, HEAD:], kv[block, HEAD:, HEAD:]], axis=1)
        values = jnp.concatenate([values, ones], axis=0)
        for at in range(0, 2048, WIDE):
            at = slice(at, at + WIDE)
            mixed = jnp.dot(values, weight[turn, :, at], preferred_element_type=F32)
            state[:, at] = state[:, at] * factor[turn, :1, at] + mixed

    state[...] = jnp.zeros_like(state)
    top[...] = jnp.full_like(top, masked_score)
    weight[1] = jnp.zeros_like(weight[1])
    factor[1] = jnp.ones_like(factor[1])
    scores(chip, 0, True)

    def compute(i, carry):
        count, last, second = carry
        block = block_at(looked_up(i))
        wanted = (block < chip) & (block >= chip - REACH)
        for turn in range(2):

            @pl.when(wanted & (lax.rem(count, 2) != turn))
            def _():
                scores(block, turn)
                softmax(1 - turn)
                mix(second, turn)

        return jnp.where(wanted, count + 1, count), jnp.where(wanted, block, last), jnp.where(wanted, last, second)

    def slot(t, carry):
        before = jnp.maximum(t - LAG, 0)
        for w in range(6):

            @pl.when(set_in(takes[w], before) & (t >= LAG))
            def _():
                hop(before, w, block_at(looked_up(before * 6 + w))).wait_recv()

        for w in range(6):

            @pl.when(set_in(gives[w], t))
            def _():
                hop(t, w, block_at(looked_up(t * 6 + w), ways[w])).start()

        first = before * 6
        return lax.fori_loop(first, jnp.where(t >= LAG, first + 6, first), compute, carry)

    count, last, second = lax.fori_loop(1, SLOTS + LAG, slot, (jnp.int32(0), chip, chip))
    for turn in range(2):

        @pl.when(lax.rem(count, 2) == turn)
        def _():
            softmax(turn)
            mix(second, 1 - turn)
            mix(last, turn)

    load_o.wait()
    for h in range(8):
        at = slice(h * ROWS, (h + 1) * ROWS)
        x = state[:HEAD, at] * (1.0 / state[HEAD : HEAD + 1, at])
        attended[:, h * HEAD : (h + 1) * HEAD] = x.T.astype(BF16)
    theirs = pl.ds(pl.multiple_of((1 - server) * HEAD, HEAD), HEAD)
    mine = pl.ds(pl.multiple_of(server * HEAD, HEAD), HEAD)
    swaps = []
    for n in range(4):
        at = slice(n * 512, (n + 1) * 512)
        sent[n] = jnp.dot(attended[theirs, :], wo[:, at], preferred_element_type=F32).astype(BF16)
        swap = pltpu.make_async_remote_copy(
            src_ref=sent.at[n],
            dst_ref=received.at[n],
            send_sem=swap_sem.at[0, n],
            recv_sem=swap_sem.at[1, n],
            device_id={"srv": 1 - server},
            device_id_type=MESH,
        )
        swap.start()
        swaps.append(swap)
    for n in range(4):
        at = slice(n * 512, (n + 1) * 512)
        part = jnp.dot(attended[mine, :], wo[:, at], preferred_element_type=F32)
        swaps[n].wait_recv()
        out[:, at] = (part + received[n].astype(F32)).astype(BF16)
    for n in range(4):
        swaps[n].wait_send()

    def left(t, carry):
        for w in range(6):

            @pl.when(set_in(gives[w], t))
            def _():
                hop(t, w, chip).wait_send()

        return carry

    lax.fori_loop(0, SLOTS, left, 0)


def local(
    tokens, norm_gain, q_gain, k_gain, w_query, w_key, w_value, w_out, doc_lengths, stretch_offsets
):
    half = jnp.arange(HEAD // 2, dtype=F32)
    frequency = rope_base ** (-2.0 * jnp.concatenate([half, half]) / HEAD)
    vmem = pl.BlockSpec(memory_space=pltpu.VMEM)
    smem = pl.BlockSpec(memory_space=pltpu.SMEM)
    hbm = pl.BlockSpec(memory_space=pl.ANY)
    dma = pltpu.SemaphoreType.DMA
    return pl.pallas_call(
        kernel,
        out_shape=jax.ShapeDtypeStruct((HEAD, 2048), BF16),
        in_specs=[hbm, vmem, vmem, vmem, vmem, hbm, hbm, hbm, hbm, smem, smem],
        out_specs=vmem,
        scratch_shapes=[
            pltpu.VMEM((ROWS, 2048), BF16),
            pltpu.VMEM((ROWS, 2048), BF16),
            pltpu.VMEM((2048, 256), BF16),
            pltpu.VMEM((4, 2048, 256), BF16),
            pltpu.VMEM((1024, 2048), BF16),
            pltpu.VMEM((BLOCKS, ROWS, 256), BF16),
            pltpu.VMEM((256, 2048), BF16),
            pltpu.VMEM((2, ROWS, 2048), F32),
            pltpu.VMEM((2, 8, 2048), F32),
            pltpu.VMEM((2, ROWS, 2048), BF16),
            pltpu.VMEM((2, 8, 2048), F32),
            pltpu.VMEM((HEAD + 16, 2048), F32),
            pltpu.VMEM((8, 2048), F32),
            pltpu.VMEM((ROWS, 1024), BF16),
            pltpu.VMEM((4, HEAD, 512), BF16),
            pltpu.VMEM((4, HEAD, 512), BF16),
            dma((4,)),
            dma((4,)),
            dma((SLOTS * 6,)),
            dma((SLOTS * 6,)),
            dma((2, 4)),
        ],
        compiler_params=pltpu.CompilerParams(
            collective_id=0, has_side_effects=True, vmem_limit_bytes=60 * 2**20
        ),
        name="attention_layer",
    )(
        tokens,
        norm_gain.reshape(1, -1),
        q_gain.reshape(1, -1),
        k_gain.reshape(1, -1),
        frequency.reshape(1, -1),
        w_query,
        w_key,
        w_value,
        w_out,
        doc_lengths,
        stretch_offsets,
    )


def solution(mesh):
    return jax.shard_map(
        local,
        mesh=mesh,
        in_specs=(
            P("ctx", None),
            P(),
            P(),
            P(),
            P(None, "srv"),
            P(),
            P(),
            P("srv", None),
            P(),
            P("ctx"),
        ),
        out_specs=P(("ctx", "srv"), None),
        check_vma=False,
    )
```

```python
import math

import jax
import jax.numpy as jnp
import numpy as np
from jax import lax
from jax.experimental import pallas as pl
from jax.experimental.pallas import tpu as pltpu
from jax.sharding import PartitionSpec as P

rope_base = 1000000.0
norm_eps = 1e-06
masked_score = -1e30
HEAD = 128
ROWS = 256
BLOCKS = 64
REACH = 40
WIDE = 512
MESH = pl.DeviceIdType.MESH
F32 = jnp.float32
BF16 = jnp.bfloat16

hop_table = (
    (16, 48, 4, 12, 1, 3),
    (0, 0, 0, 0, 0, 0),
    (17, 52, 8, 28, 5, 7),
    (0, 32, 20, 60, 49, 19),
    (21, 53, 11, 29, 6, 55),
    (35, 36, 56, 31, 9, 2),
    (27, 37, 59, 24, 18, 10),
    (47, 57, 39, 25, 61, 34),
    (23, 54, 41, 30, 22, 15),
    (43, 50, 38, 46, 26, 0),
    (45, 63, 58, 13, 62, 14),
    (40, 51, 0, 44, 33, 42),
)

ways = ((1, 0, 0), (3, 0, 0), (0, 1, 0), (0, 3, 0), (0, 0, 1), (0, 0, 3))


def apart(index):
    return (index // 16, index // 4 % 4, index % 4)


def joined(a, b, sign=1):
    y, z, x = ((p + sign * q) % 4 for p, q in zip(a, b))
    return y * 16 + z * 4 + x


SLOTS = len(hop_table)
LAG = 2


def plan():
    hops = {d: (s, w) for s, row in enumerate(hop_table) for w, d in enumerate(row) if d}
    carried = {
        at: [0 <= c - joined(apart(c), apart(d), -1) <= REACH for c in range(BLOCKS)] for d, at in hops.items()
    }
    for d, (s, w) in sorted(hops.items(), key=lambda hop: -hop[1][0]):
        parent = joined(apart(d), ways[w], -1)
        if parent:
            for c in range(BLOCKS):
                if carried[s, w][joined(apart(c), ways[w])]:
                    carried[hops[parent]][c] = True
    return carried


carried_at = plan()


def looked_up(i):
    flat = [d for row in hop_table for d in row]
    words = [sum(d << 6 * k for k, d in enumerate(flat[at : at + 5])) for at in range(0, len(flat), 5)]
    word, group = jnp.int32(words[0]), i // 5
    for k in range(1, len(words)):
        word = jnp.where(group == k, jnp.int32(words[k]), word)
    return lax.shift_right_logical(word, 6 * lax.rem(i, 5)) & 63


def spans(row):
    out, start = [], None
    for c in range(BLOCKS + 1):
        inside = c < BLOCKS and row[c]
        if inside and start is None:
            start = c
        if not inside and start is not None:
            out.append((start, c - 1))
            start = None
    return out


def among(row, chip):
    found = None
    for first, last in spans(row):
        one = (chip >= first) & (chip <= last)
        found = one if found is None else found | one
    return chip < 0 if found is None else found


def sine_cosine(angle):
    turns = jnp.floor(angle * (2.0 / math.pi) + 0.5)
    rest = angle
    for part in quarter_parts:
        rest = rest - turns * part
    square = rest * rest
    s = rest + rest * square * (
        -1.6666666666e-1 + square * (8.3333331876e-3 + square * (-1.9841270114e-4 + square * 2.7557314e-6))
    )
    c = 1.0 + square * (
        -0.5 + square * (4.16666666e-2 + square * (-1.3888888e-3 + square * (2.4801587e-5 - square * 2.7557e-7)))
    )
    quarter = turns.astype(jnp.int32) & 3
    odd = (quarter & 1) == 1
    sine, cosine = jnp.where(odd, c, s), jnp.where(odd, s, c)
    sine = jnp.where(quarter >= 2, -sine, sine)
    cosine = jnp.where((quarter == 1) | (quarter == 2), -cosine, cosine)
    return sine, cosine


def split_quarter():
    parts, left = [], math.pi / 2
    for _ in range(3):
        exponent = math.floor(math.log2(left))
        unit = 2.0 ** (exponent - 7)
        part = math.floor(left / unit) * unit
        parts.append(part)
        left -= part
    return (*parts, left)


quarter_parts = split_quarter()
score_scale_2 = math.log2(math.e) * HEAD ** (-0.5)


def scaled_and_rotated(x, gain, sine, cosine):
    x = x * lax.rsqrt(jnp.mean(x * x, axis=0, keepdims=True) + norm_eps) * gain
    a, b = x[:64], x[64:]
    return jnp.concatenate([a * cosine - b * sine, b * cosine + a * sine], axis=0)


def column(row_vector):
    square = jnp.broadcast_to(row_vector, (HEAD, HEAD)).T
    return jnp.concatenate([square, square], axis=1)


def kernel(
    tokens, norm_gain, q_gain, k_gain, frequency, w_query, w_key, w_value, w_out, doc_lengths, offsets,
    out, x_buf, normed, wkv, wq, wo, kv, q_t, score, peak, weight, factor, state, top, attended, sent, received,
    load_sem, q_sem, send_sem, recv_sem, swap_sem,
):
    chip, server = lax.axis_index("ctx"), lax.axis_index("srv")
    cy, cz, cx = chip // 16, lax.rem(chip // 4, 4), lax.rem(chip, 4)

    def moved(step, sign=1):
        dy, dz, dx = step
        if sign < 0:
            dy, dz, dx = (4 - dy) % 4, (4 - dz) % 4, (4 - dx) % 4
        return lax.rem(cy + dy, 4) * 16 + lax.rem(cz + dz, 4) * 4 + lax.rem(cx + dx, 4)

    neighbours = [moved(w) for w in ways]
    barrier = pltpu.get_barrier_semaphore()
    for n in neighbours:
        pl.semaphore_signal(barrier, inc=1, device_id={"ctx": n}, device_id_type=MESH)
    pl.semaphore_signal(barrier, inc=1, device_id={"srv": 1 - server}, device_id_type=MESH)

    lanes = pl.ds(pl.multiple_of(server * HEAD, HEAD), HEAD)
    load_x = pltpu.make_async_copy(tokens, x_buf, load_sem.at[0])
    load_k = pltpu.make_async_copy(w_key.at[:, lanes], wkv.at[:, :HEAD], load_sem.at[1])
    load_v = pltpu.make_async_copy(w_value.at[:, lanes], wkv.at[:, HEAD:], load_sem.at[2])
    load_o = pltpu.make_async_copy(w_out, wo, load_sem.at[3])
    load_q = [
        pltpu.make_async_copy(w_query.at[:, i * 256 : (i + 1) * 256], wq.at[i], q_sem.at[i]) for i in range(4)
    ]
    for copy in (load_x, load_k, load_v, *load_q, load_o):
        copy.start()

    offset = offsets[0]
    token_lane = lax.broadcasted_iota(jnp.int32, (8, ROWS), 1)
    position = (token_lane + offset).astype(F32)[:1]
    sine, cosine = sine_cosine(column(frequency[...])[:64] * jnp.broadcast_to(position, (64, ROWS)))
    lengths = [doc_lengths[i] for i in range(4)]
    ends = [lengths[0]]
    for i in range(1, 4):
        ends.append(ends[-1] + lengths[i])
    starts = [jnp.int32(0), *ends[:3]]
    feature = lax.broadcasted_iota(jnp.int32, (1, HEAD), 1)
    first_of = jnp.full((1, HEAD), 1 << 30, jnp.int32)
    end_of = jnp.full((1, HEAD), 1 << 30, jnp.int32)
    for i in range(4):
        first_of = jnp.where(feature == i, starts[i], first_of)
        end_of = jnp.where(feature == i, ends[i], end_of)
    feature_row = lax.broadcasted_iota(jnp.int32, (HEAD, ROWS), 0)
    token = lax.broadcasted_iota(jnp.int32, (HEAD, ROWS), 1) + chip * ROWS
    barred = jnp.zeros((HEAD, ROWS), F32)
    for i in range(4):
        outside = (token < starts[i]) | (token >= ends[i])
        barred = jnp.where((feature_row == i) & outside, masked_score, barred)
    barred = barred.astype(BF16)
    for h in range(8):
        q_t[HEAD:, h * ROWS : (h + 1) * ROWS] = barred

    load_x.wait()

    def norm_rows(i, carry):
        at = pl.ds(pl.multiple_of(i * 32, 32), 32)
        x = x_buf[at, :].astype(F32)
        x = x * lax.rsqrt(jnp.mean(x * x, axis=1, keepdims=True) + norm_eps) * norm_gain[...]
        normed[at, :] = x.astype(BF16)
        return carry

    lax.fori_loop(0, 8, norm_rows, 0)

    load_k.wait()
    load_v.wait()
    pair = jnp.dot(normed[...], wkv[...], preferred_element_type=F32)
    key = scaled_and_rotated(pair[:, :HEAD].T, column(k_gain[...]), sine, cosine).T.astype(BF16)
    value = pair[:, HEAD:].T.astype(BF16)
    kv[chip, :, :HEAD] = key
    kv[chip, :HEAD, HEAD:] = value[:, :HEAD]
    kv[chip, HEAD:, HEAD:] = value[:, HEAD:]

    def gathered(w, at):
        bits = jnp.int32(0)
        for t in range(SLOTS):
            if (t, w) in carried_at:
                bits += jnp.where(among(carried_at[t, w], at), 1 << t, 0)
        return bits

    takes = [gathered(w, chip) for w in range(6)]
    gives = [gathered(w, neighbours[w]) for w in range(6)]

    def set_in(bits, t):
        return lax.rem(lax.shift_right_logical(bits, t), 2) == 1

    def behind(y, z, x):
        return lax.rem(y + 4, 4) * 16 + lax.rem(z + 4, 4) * 4 + lax.rem(x + 4, 4)

    def hop(t, w, block):
        return pltpu.make_async_remote_copy(
            src_ref=kv.at[block],
            dst_ref=kv.at[block],
            send_sem=send_sem.at[t * 6 + w],
            recv_sem=recv_sem.at[t * 6 + w],
            device_id={"ctx": neighbours[w]},
            device_id_type=MESH,
        )

    def block_at(d, way=(0, 0, 0)):
        uy, uz, ux = (u - 4 * (u == 3) for u in way)
        return behind(cy - d // 16 + uy, cz - lax.rem(d // 4, 4) + uz, cx - lax.rem(d, 4) + ux)

    pl.semaphore_wait(barrier, 7)
    for w in range(6):

        @pl.when(set_in(gives[w], 0))
        def _():
            hop(0, w, chip).start()


    q_column = column(q_gain[...])
    for i in range(4):
        load_q[i].wait()
        two = jnp.dot(normed[...], wq[i], preferred_element_type=F32)
        for u in range(2):
            h = 2 * i + u
            x = scaled_and_rotated(two[:, u * HEAD : (u + 1) * HEAD].T, q_column, sine, cosine)
            q_t[:HEAD, h * ROWS : (h + 1) * ROWS] = x.astype(BF16)

    ones = jnp.ones((16, ROWS), BF16)

    def keys_of(block):
        key_at = lax.broadcasted_iota(jnp.int32, (ROWS, HEAD), 0) + block * ROWS
        segment = jnp.where((key_at >= first_of) & (key_at < end_of), 1.0, 0.0).astype(BF16)
        return jnp.concatenate([kv[block, :, :HEAD], segment], axis=1)

    def values_of(block):
        values = jnp.concatenate([kv[block, :HEAD, HEAD:], kv[block, HEAD:, HEAD:]], axis=1)
        return jnp.concatenate([values, ones], axis=0)

    def scores(keys, turn, at, own=False):
        s = jnp.dot(keys, q_t[:, at], preferred_element_type=F32)
        if own:
            later = lax.broadcasted_iota(jnp.int32, s.shape, 0) > lax.broadcasted_iota(jnp.int32, s.shape, 1)
            s = jnp.where(later, masked_score, s)
        score[turn, :, at] = s
        peak[turn, :, at] = jnp.max(s.reshape(ROWS // 8, 8, -1), axis=0)

    def softmax(turn, at):
        before = top[:, at]
        highest = jnp.maximum(before, jnp.max(peak[turn, :, at], axis=0, keepdims=True) * score_scale_2)
        top[:, at] = highest
        factor[turn, :, at] = jnp.exp2(before - highest)
        weight[turn, :, at] = jnp.exp2(score[turn, :, at] * score_scale_2 - highest[:1]).astype(BF16)

    def mix(values, turn, at):
        mixed = jnp.dot(values, weight[turn, :, at], preferred_element_type=F32)
        state[:, at] = state[:, at] * factor[turn, :1, at] + mixed

    groups = [slice(at, at + WIDE) for at in range(0, 2048, WIDE)]

    state[...] = jnp.zeros_like(state)
    top[...] = jnp.full_like(top, masked_score)
    weight[1] = jnp.zeros_like(weight[1])
    factor[1] = jnp.ones_like(factor[1])
    own_keys = keys_of(chip)
    for h in range(8):
        scores(own_keys, 0, slice(h * ROWS, (h + 1) * ROWS), True)

    def compute(i, carry):
        count, last, second = carry
        block = block_at(looked_up(i))
        wanted = (block < chip) & (block >= chip - REACH)
        for turn in range(2):

            @pl.when(wanted & (lax.rem(count, 2) != turn))
            def _():
                keys, values = keys_of(block), values_of(second)
                for at in groups:
                    scores(keys, turn, at)
                    softmax(1 - turn, at)
                    mix(values, turn, at)

        return jnp.where(wanted, count + 1, count), jnp.where(wanted, block, last), jnp.where(wanted, last, second)

    def slot(t, carry):
        before = jnp.maximum(t - LAG, 0)
        for w in range(6):

            @pl.when(set_in(takes[w], before) & (t >= LAG))
            def _():
                hop(before, w, block_at(looked_up(before * 6 + w))).wait_recv()

        for w in range(6):

            @pl.when(set_in(gives[w], t))
            def _():
                hop(t, w, block_at(looked_up(t * 6 + w), ways[w])).start()

        first = before * 6
        return lax.fori_loop(first, jnp.where(t >= LAG, first + 6, first), compute, carry)

    count, last, second = lax.fori_loop(1, SLOTS + LAG, slot, (jnp.int32(0), chip, chip))
    for turn in range(2):

        @pl.when(lax.rem(count, 2) == turn)
        def _():
            before, now = values_of(second), values_of(last)
            for at in groups:
                softmax(turn, at)
                mix(before, 1 - turn, at)
                mix(now, turn, at)

    load_o.wait()
    for h in range(8):
        at = slice(h * ROWS, (h + 1) * ROWS)
        x = state[:HEAD, at] * (1.0 / state[HEAD : HEAD + 1, at])
        attended[:, h * HEAD : (h + 1) * HEAD] = x.T.astype(BF16)
    theirs = pl.ds(pl.multiple_of((1 - server) * HEAD, HEAD), HEAD)
    mine = pl.ds(pl.multiple_of(server * HEAD, HEAD), HEAD)
    swaps = []
    for n in range(4):
        at = slice(n * 512, (n + 1) * 512)
        sent[n] = jnp.dot(attended[theirs, :], wo[:, at], preferred_element_type=F32).astype(BF16)
        swap = pltpu.make_async_remote_copy(
            src_ref=sent.at[n],
            dst_ref=received.at[n],
            send_sem=swap_sem.at[0, n],
            recv_sem=swap_sem.at[1, n],
            device_id={"srv": 1 - server},
            device_id_type=MESH,
        )
        swap.start()
        swaps.append(swap)
    for n in range(4):
        at = slice(n * 512, (n + 1) * 512)
        part = jnp.dot(attended[mine, :], wo[:, at], preferred_element_type=F32)
        swaps[n].wait_recv()
        out[:, at] = (part + received[n].astype(F32)).astype(BF16)
    for n in range(4):
        swaps[n].wait_send()

    def left(t, carry):
        for w in range(6):

            @pl.when(set_in(gives[w], t))
            def _():
                hop(t, w, chip).wait_send()

        return carry

    lax.fori_loop(0, SLOTS, left, 0)


def local(
    tokens, norm_gain, q_gain, k_gain, w_query, w_key, w_value, w_out, doc_lengths, stretch_offsets
):
    half = jnp.arange(HEAD // 2, dtype=F32)
    frequency = rope_base ** (-2.0 * jnp.concatenate([half, half]) / HEAD)
    vmem = pl.BlockSpec(memory_space=pltpu.VMEM)
    smem = pl.BlockSpec(memory_space=pltpu.SMEM)
    hbm = pl.BlockSpec(memory_space=pl.ANY)
    dma = pltpu.SemaphoreType.DMA
    return pl.pallas_call(
        kernel,
        out_shape=jax.ShapeDtypeStruct((HEAD, 2048), BF16),
        in_specs=[hbm, vmem, vmem, vmem, vmem, hbm, hbm, hbm, hbm, smem, smem],
        out_specs=vmem,
        scratch_shapes=[
            pltpu.VMEM((ROWS, 2048), BF16),
            pltpu.VMEM((ROWS, 2048), BF16),
            pltpu.VMEM((2048, 256), BF16),
            pltpu.VMEM((4, 2048, 256), BF16),
            pltpu.VMEM((1024, 2048), BF16),
            pltpu.VMEM((BLOCKS, ROWS, 256), BF16),
            pltpu.VMEM((256, 2048), BF16),
            pltpu.VMEM((2, ROWS, 2048), F32),
            pltpu.VMEM((2, 8, 2048), F32),
            pltpu.VMEM((2, ROWS, 2048), BF16),
            pltpu.VMEM((2, 8, 2048), F32),
            pltpu.VMEM((HEAD + 16, 2048), F32),
            pltpu.VMEM((8, 2048), F32),
            pltpu.VMEM((ROWS, 1024), BF16),
            pltpu.VMEM((4, HEAD, 512), BF16),
            pltpu.VMEM((4, HEAD, 512), BF16),
            dma((4,)),
            dma((4,)),
            dma((SLOTS * 6,)),
            dma((SLOTS * 6,)),
            dma((2, 4)),
        ],
        compiler_params=pltpu.CompilerParams(
            collective_id=0, has_side_effects=True, vmem_limit_bytes=60 * 2**20
        ),
        name="attention_layer",
    )(
        tokens,
        norm_gain.reshape(1, -1),
        q_gain.reshape(1, -1),
        k_gain.reshape(1, -1),
        frequency.reshape(1, -1),
        w_query,
        w_key,
        w_value,
        w_out,
        doc_lengths,
        stretch_offsets,
    )


def solution(mesh):
    return jax.shard_map(
        local,
        mesh=mesh,
        in_specs=(
            P("ctx", None),
            P(),
            P(),
            P(),
            P(None, "srv"),
            P(),
            P(),
            P("srv", None),
            P(),
            P("ctx"),
        ),
        out_specs=P(("ctx", "srv"), None),
        check_vma=False,
    )
```

```python
import math

import jax
import jax.numpy as jnp
import numpy as np
from jax import lax
from jax.experimental import pallas as pl
from jax.experimental.pallas import tpu as pltpu
from jax.sharding import PartitionSpec as P

rope_base = 1000000.0
norm_eps = 1e-06
masked_score = -1e30
HEAD = 128
ROWS = 256
BLOCKS = 64
REACH = 40
WIDE = 512
MESH = pl.DeviceIdType.MESH
F32 = jnp.float32
BF16 = jnp.bfloat16

hop_table = (
    (16, 48, 4, 12, 1, 3),
    (0, 0, 0, 0, 0, 0),
    (28, 52, 20, 13, 17, 7),
    (0, 32, 5, 8, 2, 19),
    (29, 60, 56, 24, 21, 31),
    (33, 55, 9, 44, 14, 18),
    (47, 49, 23, 27, 25, 6),
    (37, 39, 22, 30, 53, 63),
    (35, 40, 36, 15, 26, 46),
    (45, 57, 41, 10, 54, 38),
    (0, 51, 11, 42, 34, 43),
    (0, 50, 58, 59, 61, 62),
)

ways = ((1, 0, 0), (3, 0, 0), (0, 1, 0), (0, 3, 0), (0, 0, 1), (0, 0, 3))


def apart(index):
    return (index // 16, index // 4 % 4, index % 4)


def joined(a, b, sign=1):
    y, z, x = ((p + sign * q) % 4 for p, q in zip(a, b))
    return y * 16 + z * 4 + x


SLOTS = len(hop_table)
LAG = 2


def plan():
    hops = {d: (s, w) for s, row in enumerate(hop_table) for w, d in enumerate(row) if d}
    carried = {
        at: [0 <= c - joined(apart(c), apart(d), -1) <= REACH for c in range(BLOCKS)] for d, at in hops.items()
    }
    for d, (s, w) in sorted(hops.items(), key=lambda hop: -hop[1][0]):
        parent = joined(apart(d), ways[w], -1)
        if parent:
            for c in range(BLOCKS):
                if carried[s, w][joined(apart(c), ways[w])]:
                    carried[hops[parent]][c] = True
    return carried


carried_at = plan()


def looked_up(i):
    flat = [d for row in hop_table for d in row]
    words = [sum(d << 6 * k for k, d in enumerate(flat[at : at + 5])) for at in range(0, len(flat), 5)]
    word, group = jnp.int32(words[0]), i // 5
    for k in range(1, len(words)):
        word = jnp.where(group == k, jnp.int32(words[k]), word)
    return lax.shift_right_logical(word, 6 * lax.rem(i, 5)) & 63


def spans(row):
    out, start = [], None
    for c in range(BLOCKS + 1):
        inside = c < BLOCKS and row[c]
        if inside and start is None:
            start = c
        if not inside and start is not None:
            out.append((start, c - 1))
            start = None
    return out


def among(row, chip):
    found = None
    for first, last in spans(row):
        one = (chip >= first) & (chip <= last)
        found = one if found is None else found | one
    return chip < 0 if found is None else found


def sine_cosine(angle):
    turns = jnp.floor(angle * (2.0 / math.pi) + 0.5)
    rest = angle
    for part in quarter_parts:
        rest = rest - turns * part
    square = rest * rest
    s = rest + rest * square * (
        -1.6666666666e-1 + square * (8.3333331876e-3 + square * (-1.9841270114e-4 + square * 2.7557314e-6))
    )
    c = 1.0 + square * (
        -0.5 + square * (4.16666666e-2 + square * (-1.3888888e-3 + square * (2.4801587e-5 - square * 2.7557e-7)))
    )
    quarter = turns.astype(jnp.int32) & 3
    odd = (quarter & 1) == 1
    sine, cosine = jnp.where(odd, c, s), jnp.where(odd, s, c)
    sine = jnp.where(quarter >= 2, -sine, sine)
    cosine = jnp.where((quarter == 1) | (quarter == 2), -cosine, cosine)
    return sine, cosine


def split_quarter():
    parts, left = [], math.pi / 2
    for _ in range(3):
        exponent = math.floor(math.log2(left))
        unit = 2.0 ** (exponent - 7)
        part = math.floor(left / unit) * unit
        parts.append(part)
        left -= part
    return (*parts, left)


quarter_parts = split_quarter()
score_scale_2 = math.log2(math.e) * HEAD ** (-0.5)


def scaled_and_rotated(x, gain, sine, cosine):
    x = x * lax.rsqrt(jnp.mean(x * x, axis=0, keepdims=True) + norm_eps) * gain
    a, b = x[:64], x[64:]
    return jnp.concatenate([a * cosine - b * sine, b * cosine + a * sine], axis=0)


def column(row_vector):
    square = jnp.broadcast_to(row_vector, (HEAD, HEAD)).T
    return jnp.concatenate([square, square], axis=1)


def kernel(
    tokens, norm_gain, q_gain, k_gain, frequency, w_query, w_key, w_value, w_out, doc_lengths, offsets,
    out, x_buf, normed, wkv, wq, wo, kv, q_t, score, peak, weight, factor, state, top, attended, sent, received,
    load_sem, q_sem, send_sem, recv_sem, swap_sem,
):
    chip, server = lax.axis_index("ctx"), lax.axis_index("srv")
    cy, cz, cx = chip // 16, lax.rem(chip // 4, 4), lax.rem(chip, 4)

    def moved(step, sign=1):
        dy, dz, dx = step
        if sign < 0:
            dy, dz, dx = (4 - dy) % 4, (4 - dz) % 4, (4 - dx) % 4
        return lax.rem(cy + dy, 4) * 16 + lax.rem(cz + dz, 4) * 4 + lax.rem(cx + dx, 4)

    neighbours = [moved(w) for w in ways]
    barrier = pltpu.get_barrier_semaphore()
    for n in neighbours:
        pl.semaphore_signal(barrier, inc=1, device_id={"ctx": n}, device_id_type=MESH)
    pl.semaphore_signal(barrier, inc=1, device_id={"srv": 1 - server}, device_id_type=MESH)

    lanes = pl.ds(pl.multiple_of(server * HEAD, HEAD), HEAD)
    load_x = pltpu.make_async_copy(tokens, x_buf, load_sem.at[0])
    load_k = pltpu.make_async_copy(w_key.at[:, lanes], wkv.at[:, :HEAD], load_sem.at[1])
    load_v = pltpu.make_async_copy(w_value.at[:, lanes], wkv.at[:, HEAD:], load_sem.at[2])
    load_o = pltpu.make_async_copy(w_out, wo, load_sem.at[3])
    load_q = [
        pltpu.make_async_copy(w_query.at[:, i * 256 : (i + 1) * 256], wq.at[i], q_sem.at[i]) for i in range(4)
    ]
    for copy in (load_x, load_k, load_v, *load_q, load_o):
        copy.start()

    offset = offsets[0]
    token_lane = lax.broadcasted_iota(jnp.int32, (8, ROWS), 1)
    position = (token_lane + offset).astype(F32)[:1]
    sine, cosine = sine_cosine(column(frequency[...])[:64] * jnp.broadcast_to(position, (64, ROWS)))
    lengths = [doc_lengths[i] for i in range(4)]
    ends = [lengths[0]]
    for i in range(1, 4):
        ends.append(ends[-1] + lengths[i])
    starts = [jnp.int32(0), *ends[:3]]
    feature = lax.broadcasted_iota(jnp.int32, (1, HEAD), 1)
    first_of = jnp.full((1, HEAD), 1 << 30, jnp.int32)
    end_of = jnp.full((1, HEAD), 1 << 30, jnp.int32)
    for i in range(4):
        first_of = jnp.where(feature == i, starts[i], first_of)
        end_of = jnp.where(feature == i, ends[i], end_of)
    feature_row = lax.broadcasted_iota(jnp.int32, (HEAD, ROWS), 0)
    token = lax.broadcasted_iota(jnp.int32, (HEAD, ROWS), 1) + chip * ROWS
    barred = jnp.zeros((HEAD, ROWS), F32)
    for i in range(4):
        outside = (token < starts[i]) | (token >= ends[i])
        barred = jnp.where((feature_row == i) & outside, masked_score, barred)
    barred = barred.astype(BF16)
    for h in range(8):
        q_t[HEAD:, h * ROWS : (h + 1) * ROWS] = barred

    def gathered(w, at):
        bits = jnp.int32(0)
        for t in range(SLOTS):
            if (t, w) in carried_at:
                bits += jnp.where(among(carried_at[t, w], at), 1 << t, 0)
        return bits

    takes = [gathered(w, chip) for w in range(6)]
    gives = [gathered(w, neighbours[w]) for w in range(6)]

    load_x.wait()

    def norm_rows(i, carry):
        at = pl.ds(pl.multiple_of(i * 32, 32), 32)
        x = x_buf[at, :].astype(F32)
        x = x * lax.rsqrt(jnp.mean(x * x, axis=1, keepdims=True) + norm_eps) * norm_gain[...]
        normed[at, :] = x.astype(BF16)
        return carry

    lax.fori_loop(0, 8, norm_rows, 0)

    load_k.wait()
    load_v.wait()
    pair = jnp.dot(normed[...], wkv[...], preferred_element_type=F32)
    key = scaled_and_rotated(pair[:, :HEAD].T, column(k_gain[...]), sine, cosine).T.astype(BF16)
    value = pair[:, HEAD:].T.astype(BF16)
    kv[chip, :, :HEAD] = key
    kv[chip, :HEAD, HEAD:] = value[:, :HEAD]
    kv[chip, HEAD:, HEAD:] = value[:, HEAD:]

    def set_in(bits, t):
        return lax.rem(lax.shift_right_logical(bits, t), 2) == 1

    def behind(y, z, x):
        return lax.rem(y + 4, 4) * 16 + lax.rem(z + 4, 4) * 4 + lax.rem(x + 4, 4)

    def hop(t, w, block):
        return pltpu.make_async_remote_copy(
            src_ref=kv.at[block],
            dst_ref=kv.at[block],
            send_sem=send_sem.at[t * 6 + w],
            recv_sem=recv_sem.at[t * 6 + w],
            device_id={"ctx": neighbours[w]},
            device_id_type=MESH,
        )

    def block_at(d, way=(0, 0, 0)):
        uy, uz, ux = (u - 4 * (u == 3) for u in way)
        return behind(cy - d // 16 + uy, cz - lax.rem(d // 4, 4) + uz, cx - lax.rem(d, 4) + ux)

    pl.semaphore_wait(barrier, 7)
    for w in range(6):

        @pl.when(set_in(gives[w], 0))
        def _():
            hop(0, w, chip).start()


    q_column = column(q_gain[...])
    for i in range(4):
        load_q[i].wait()
        two = jnp.dot(normed[...], wq[i], preferred_element_type=F32)
        for u in range(2):
            h = 2 * i + u
            x = scaled_and_rotated(two[:, u * HEAD : (u + 1) * HEAD].T, q_column, sine, cosine)
            q_t[:HEAD, h * ROWS : (h + 1) * ROWS] = x.astype(BF16)

    ones = jnp.ones((16, ROWS), BF16)

    def keys_of(block):
        key_at = lax.broadcasted_iota(jnp.int32, (ROWS, HEAD), 0) + block * ROWS
        segment = jnp.where((key_at >= first_of) & (key_at < end_of), 1.0, 0.0).astype(BF16)
        return jnp.concatenate([kv[block, :, :HEAD], segment], axis=1)

    def values_of(block):
        values = jnp.concatenate([kv[block, :HEAD, HEAD:], kv[block, HEAD:, HEAD:]], axis=1)
        return jnp.concatenate([values, ones], axis=0)

    def scores(keys, turn, at, own=False):
        s = jnp.dot(keys, q_t[:, at], preferred_element_type=F32)
        if own:
            later = lax.broadcasted_iota(jnp.int32, s.shape, 0) > lax.broadcasted_iota(jnp.int32, s.shape, 1)
            s = jnp.where(later, masked_score, s)
        score[turn, :, at] = s
        peak[turn, :, at] = jnp.max(s.reshape(ROWS // 8, 8, -1), axis=0)

    def softmax(turn, at):
        before = top[:, at]
        highest = jnp.maximum(before, jnp.max(peak[turn, :, at], axis=0, keepdims=True) * score_scale_2)
        top[:, at] = highest
        factor[turn, :, at] = jnp.exp2(before - highest)
        weight[turn, :, at] = jnp.exp2(score[turn, :, at] * score_scale_2 - highest[:1]).astype(BF16)

    def mix(values, turn, at):
        mixed = jnp.dot(values, weight[turn, :, at], preferred_element_type=F32)
        state[:, at] = state[:, at] * factor[turn, :1, at] + mixed

    groups = [slice(at, at + WIDE) for at in range(0, 2048, WIDE)]

    state[...] = jnp.zeros_like(state)
    top[...] = jnp.full_like(top, masked_score)
    weight[1] = jnp.zeros_like(weight[1])
    factor[1] = jnp.ones_like(factor[1])
    own_keys = keys_of(chip)
    for h in range(8):
        scores(own_keys, 0, slice(h * ROWS, (h + 1) * ROWS), True)

    def compute(i, carry):
        count, last, second = carry
        block = block_at(looked_up(i))
        wanted = (block < chip) & (block >= chip - REACH)
        for turn in range(2):

            @pl.when(wanted & (lax.rem(count, 2) != turn))
            def _():
                keys, values = keys_of(block), values_of(second)
                for at in groups:
                    scores(keys, turn, at)
                    softmax(1 - turn, at)
                    mix(values, turn, at)

        return jnp.where(wanted, count + 1, count), jnp.where(wanted, block, last), jnp.where(wanted, last, second)

    def slot(t, carry):
        before = jnp.maximum(t - LAG, 0)
        for w in range(6):

            @pl.when(set_in(takes[w], before) & (t >= LAG))
            def _():
                hop(before, w, block_at(looked_up(before * 6 + w))).wait_recv()

        for w in range(6):

            @pl.when(set_in(gives[w], t))
            def _():
                hop(t, w, block_at(looked_up(t * 6 + w), ways[w])).start()

        first = before * 6
        return lax.fori_loop(first, jnp.where(t >= LAG, first + 6, first), compute, carry)

    count, last, second = lax.fori_loop(1, SLOTS + LAG, slot, (jnp.int32(0), chip, chip))
    for turn in range(2):

        @pl.when(lax.rem(count, 2) == turn)
        def _():
            before, now = values_of(second), values_of(last)
            for at in groups:
                softmax(turn, at)
                mix(before, 1 - turn, at)
                mix(now, turn, at)

    load_o.wait()
    for h in range(8):
        at = slice(h * ROWS, (h + 1) * ROWS)
        x = state[:HEAD, at] * (1.0 / state[HEAD : HEAD + 1, at])
        attended[:, h * HEAD : (h + 1) * HEAD] = x.T.astype(BF16)
    theirs = pl.ds(pl.multiple_of((1 - server) * HEAD, HEAD), HEAD)
    mine = pl.ds(pl.multiple_of(server * HEAD, HEAD), HEAD)
    swaps = []
    for n in range(4):
        at = slice(n * 512, (n + 1) * 512)
        sent[n] = jnp.dot(attended[theirs, :], wo[:, at], preferred_element_type=F32).astype(BF16)
        swap = pltpu.make_async_remote_copy(
            src_ref=sent.at[n],
            dst_ref=received.at[n],
            send_sem=swap_sem.at[0, n],
            recv_sem=swap_sem.at[1, n],
            device_id={"srv": 1 - server},
            device_id_type=MESH,
        )
        swap.start()
        swaps.append(swap)
    for n in range(4):
        at = slice(n * 512, (n + 1) * 512)
        part = jnp.dot(attended[mine, :], wo[:, at], preferred_element_type=F32)
        swaps[n].wait_recv()
        out[:, at] = part + received[n].astype(F32)
    for n in range(4):
        swaps[n].wait_send()

    def left(t, carry):
        for w in range(6):

            @pl.when(set_in(gives[w], t))
            def _():
                hop(t, w, chip).wait_send()

        return carry

    lax.fori_loop(0, SLOTS, left, 0)


def local(
    tokens, norm_gain, q_gain, k_gain, w_query, w_key, w_value, w_out, doc_lengths, stretch_offsets
):
    half = jnp.arange(HEAD // 2, dtype=F32)
    frequency = rope_base ** (-2.0 * jnp.concatenate([half, half]) / HEAD)
    vmem = pl.BlockSpec(memory_space=pltpu.VMEM)
    smem = pl.BlockSpec(memory_space=pltpu.SMEM)
    hbm = pl.BlockSpec(memory_space=pl.ANY)
    dma = pltpu.SemaphoreType.DMA
    summed = pl.pallas_call(
        kernel,
        out_shape=jax.ShapeDtypeStruct((HEAD, 2048), F32),
        in_specs=[hbm, vmem, vmem, vmem, vmem, hbm, hbm, hbm, hbm, smem, smem],
        out_specs=vmem,
        scratch_shapes=[
            pltpu.VMEM((ROWS, 2048), BF16),
            pltpu.VMEM((ROWS, 2048), BF16),
            pltpu.VMEM((2048, 256), BF16),
            pltpu.VMEM((4, 2048, 256), BF16),
            pltpu.VMEM((1024, 2048), BF16),
            pltpu.VMEM((BLOCKS, ROWS, 256), BF16),
            pltpu.VMEM((256, 2048), BF16),
            pltpu.VMEM((2, ROWS, 2048), F32),
            pltpu.VMEM((2, 8, 2048), F32),
            pltpu.VMEM((2, ROWS, 2048), BF16),
            pltpu.VMEM((2, 8, 2048), F32),
            pltpu.VMEM((HEAD + 16, 2048), F32),
            pltpu.VMEM((8, 2048), F32),
            pltpu.VMEM((ROWS, 1024), BF16),
            pltpu.VMEM((4, HEAD, 512), BF16),
            pltpu.VMEM((4, HEAD, 512), BF16),
            dma((4,)),
            dma((4,)),
            dma((SLOTS * 6,)),
            dma((SLOTS * 6,)),
            dma((2, 4)),
        ],
        compiler_params=pltpu.CompilerParams(
            collective_id=0, has_side_effects=True, vmem_limit_bytes=60 * 2**20
        ),
        name="attention_layer",
    )(
        tokens,
        norm_gain.reshape(1, -1),
        q_gain.reshape(1, -1),
        k_gain.reshape(1, -1),
        frequency.reshape(1, -1),
        w_query,
        w_key,
        w_value,
        w_out,
        doc_lengths,
        stretch_offsets,
    )
    return summed.astype(BF16)


def solution(mesh):
    return jax.shard_map(
        local,
        mesh=mesh,
        in_specs=(
            P("ctx", None),
            P(),
            P(),
            P(),
            P(None, "srv"),
            P(),
            P(),
            P("srv", None),
            P(),
            P("ctx"),
        ),
        out_specs=P(("ctx", "srv"), None),
        check_vma=False,
    )
```

```python
import math

import jax
import jax.numpy as jnp
import numpy as np
from jax import lax
from jax.experimental import pallas as pl
from jax.experimental.pallas import tpu as pltpu
from jax.sharding import PartitionSpec as P

rope_base = 1000000.0
norm_eps = 1e-06
masked_score = -1e30
HEAD = 128
ROWS = 256
BLOCKS = 64
REACH = 40
WIDE = 512
MESH = pl.DeviceIdType.MESH
F32 = jnp.float32
BF16 = jnp.bfloat16

hop_table = (
    (16, 48, 4, 12, 1, 3),
    (0, 0, 0, 0, 0, 0),
    (28, 52, 20, 13, 17, 7),
    (0, 32, 5, 8, 2, 19),
    (29, 60, 56, 24, 21, 31),
    (33, 55, 9, 44, 14, 18),
    (47, 49, 23, 27, 25, 6),
    (37, 39, 22, 30, 53, 63),
    (35, 40, 36, 15, 26, 46),
    (45, 57, 41, 10, 54, 38),
    (0, 51, 11, 42, 34, 43),
    (0, 50, 58, 59, 61, 62),
)

ways = ((1, 0, 0), (3, 0, 0), (0, 1, 0), (0, 3, 0), (0, 0, 1), (0, 0, 3))


def apart(index):
    return (index // 16, index // 4 % 4, index % 4)


def joined(a, b, sign=1):
    y, z, x = ((p + sign * q) % 4 for p, q in zip(a, b))
    return y * 16 + z * 4 + x


SLOTS = len(hop_table)
LAG = 2


def plan():
    hops = {d: (s, w) for s, row in enumerate(hop_table) for w, d in enumerate(row) if d}
    carried = {
        at: [0 <= c - joined(apart(c), apart(d), -1) <= REACH for c in range(BLOCKS)] for d, at in hops.items()
    }
    for d, (s, w) in sorted(hops.items(), key=lambda hop: -hop[1][0]):
        parent = joined(apart(d), ways[w], -1)
        if parent:
            for c in range(BLOCKS):
                if carried[s, w][joined(apart(c), ways[w])]:
                    carried[hops[parent]][c] = True
    return carried


carried_at = plan()


def looked_up(i):
    flat = [d for row in hop_table for d in row]
    words = [sum(d << 6 * k for k, d in enumerate(flat[at : at + 5])) for at in range(0, len(flat), 5)]
    word, group = jnp.int32(words[0]), i // 5
    for k in range(1, len(words)):
        word = jnp.where(group == k, jnp.int32(words[k]), word)
    return lax.shift_right_logical(word, 6 * lax.rem(i, 5)) & 63


def spans(row):
    out, start = [], None
    for c in range(BLOCKS + 1):
        inside = c < BLOCKS and row[c]
        if inside and start is None:
            start = c
        if not inside and start is not None:
            out.append((start, c - 1))
            start = None
    return out


def among(row, chip):
    found = None
    for first, last in spans(row):
        one = (chip >= first) & (chip <= last)
        found = one if found is None else found | one
    return chip < 0 if found is None else found


def sine_cosine(angle):
    turns = jnp.floor(angle * (2.0 / math.pi) + 0.5)
    rest = angle
    for part in quarter_parts:
        rest = rest - turns * part
    square = rest * rest
    s = rest + rest * square * (
        -1.6666666666e-1 + square * (8.3333331876e-3 + square * (-1.9841270114e-4 + square * 2.7557314e-6))
    )
    c = 1.0 + square * (
        -0.5 + square * (4.16666666e-2 + square * (-1.3888888e-3 + square * (2.4801587e-5 - square * 2.7557e-7)))
    )
    quarter = turns.astype(jnp.int32) & 3
    odd = (quarter & 1) == 1
    sine, cosine = jnp.where(odd, c, s), jnp.where(odd, s, c)
    sine = jnp.where(quarter >= 2, -sine, sine)
    cosine = jnp.where((quarter == 1) | (quarter == 2), -cosine, cosine)
    return sine, cosine


def split_quarter():
    parts, left = [], math.pi / 2
    for _ in range(3):
        exponent = math.floor(math.log2(left))
        unit = 2.0 ** (exponent - 7)
        part = math.floor(left / unit) * unit
        parts.append(part)
        left -= part
    return (*parts, left)


quarter_parts = split_quarter()
score_scale_2 = math.log2(math.e) * HEAD ** (-0.5)


def scaled_and_rotated(x, gain, sine, cosine):
    x = x * lax.rsqrt(jnp.mean(x * x, axis=0, keepdims=True) + norm_eps) * gain
    a, b = x[:64], x[64:]
    return jnp.concatenate([a * cosine - b * sine, b * cosine + a * sine], axis=0)


def column(row_vector):
    square = jnp.broadcast_to(row_vector, (HEAD, HEAD)).T
    return jnp.concatenate([square, square], axis=1)


def kernel(
    tokens, norm_gain, q_gain, k_gain, frequency, w_query, w_key, w_value, w_out, doc_lengths, offsets,
    out, x_buf, normed, wkv, wq, wo, kv, q_t, score, peak, weight, factor, state, top, attended, sent, received,
    load_sem, q_sem, send_sem, recv_sem, swap_sem,
):
    chip, server = lax.axis_index("ctx"), lax.axis_index("srv")
    cy, cz, cx = chip // 16, lax.rem(chip // 4, 4), lax.rem(chip, 4)

    def moved(step, sign=1):
        dy, dz, dx = step
        if sign < 0:
            dy, dz, dx = (4 - dy) % 4, (4 - dz) % 4, (4 - dx) % 4
        return lax.rem(cy + dy, 4) * 16 + lax.rem(cz + dz, 4) * 4 + lax.rem(cx + dx, 4)

    neighbours = [moved(w) for w in ways]
    barrier = pltpu.get_barrier_semaphore()
    for n in neighbours:
        pl.semaphore_signal(barrier, inc=1, device_id={"ctx": n}, device_id_type=MESH)
    pl.semaphore_signal(barrier, inc=1, device_id={"srv": 1 - server}, device_id_type=MESH)

    lanes = pl.ds(pl.multiple_of(server * HEAD, HEAD), HEAD)
    load_x = pltpu.make_async_copy(tokens, x_buf, load_sem.at[0])
    load_k = pltpu.make_async_copy(w_key.at[:, lanes], wkv.at[:, :HEAD], load_sem.at[1])
    load_v = pltpu.make_async_copy(w_value.at[:, lanes], wkv.at[:, HEAD:], load_sem.at[2])
    load_o = pltpu.make_async_copy(w_out, wo, load_sem.at[3])
    load_q = [
        pltpu.make_async_copy(w_query.at[:, i * 256 : (i + 1) * 256], wq.at[i], q_sem.at[i]) for i in range(4)
    ]
    for copy in (load_x, load_k, load_v, *load_q, load_o):
        copy.start()

    offset = offsets[0]
    token_lane = lax.broadcasted_iota(jnp.int32, (8, ROWS), 1)
    position = (token_lane + offset).astype(F32)[:1]
    sine, cosine = sine_cosine(column(frequency[...])[:64] * jnp.broadcast_to(position, (64, ROWS)))
    lengths = [doc_lengths[i] for i in range(4)]
    ends = [lengths[0]]
    for i in range(1, 4):
        ends.append(ends[-1] + lengths[i])
    starts = [jnp.int32(0), *ends[:3]]
    feature = lax.broadcasted_iota(jnp.int32, (1, HEAD), 1)
    first_of = jnp.full((1, HEAD), 1 << 30, jnp.int32)
    end_of = jnp.full((1, HEAD), 1 << 30, jnp.int32)
    for i in range(4):
        first_of = jnp.where(feature == i, starts[i], first_of)
        end_of = jnp.where(feature == i, ends[i], end_of)
    feature_row = lax.broadcasted_iota(jnp.int32, (HEAD, ROWS), 0)
    token = lax.broadcasted_iota(jnp.int32, (HEAD, ROWS), 1) + chip * ROWS
    barred = jnp.zeros((HEAD, ROWS), F32)
    for i in range(4):
        outside = (token < starts[i]) | (token >= ends[i])
        barred = jnp.where((feature_row == i) & outside, masked_score, barred)
    barred = barred.astype(BF16)
    for h in range(8):
        q_t[HEAD:, h * ROWS : (h + 1) * ROWS] = barred

    def gathered(w, at):
        bits = jnp.int32(0)
        for t in range(SLOTS):
            if (t, w) in carried_at:
                bits += jnp.where(among(carried_at[t, w], at), 1 << t, 0)
        return bits

    takes = [gathered(w, chip) for w in range(6)]
    gives = [gathered(w, neighbours[w]) for w in range(6)]

    load_x.wait()

    def norm_rows(i, carry):
        at = pl.ds(pl.multiple_of(i * 32, 32), 32)
        x = x_buf[at, :].astype(F32)
        x = x * lax.rsqrt(jnp.mean(x * x, axis=1, keepdims=True) + norm_eps) * norm_gain[...]
        normed[at, :] = x.astype(BF16)
        return carry

    lax.fori_loop(0, 8, norm_rows, 0)

    load_k.wait()
    load_v.wait()
    pair = jnp.dot(normed[...], wkv[...], preferred_element_type=F32)
    key = scaled_and_rotated(pair[:, :HEAD].T, column(k_gain[...]), sine, cosine).T.astype(BF16)
    value = pair[:, HEAD:].T.astype(BF16)
    kv[chip, :, :HEAD] = key
    kv[chip, :HEAD, HEAD:] = value[:, :HEAD]
    kv[chip, HEAD:, HEAD:] = value[:, HEAD:]

    def set_in(bits, t):
        return lax.rem(lax.shift_right_logical(bits, t), 2) == 1

    def behind(y, z, x):
        return lax.rem(y + 4, 4) * 16 + lax.rem(z + 4, 4) * 4 + lax.rem(x + 4, 4)

    def hop(t, w, block):
        return pltpu.make_async_remote_copy(
            src_ref=kv.at[block],
            dst_ref=kv.at[block],
            send_sem=send_sem.at[t * 6 + w],
            recv_sem=recv_sem.at[t * 6 + w],
            device_id={"ctx": neighbours[w]},
            device_id_type=MESH,
        )

    def block_at(d, way=(0, 0, 0)):
        uy, uz, ux = (u - 4 * (u == 3) for u in way)
        return behind(cy - d // 16 + uy, cz - lax.rem(d // 4, 4) + uz, cx - lax.rem(d, 4) + ux)

    pl.semaphore_wait(barrier, 7)
    for w in range(6):

        @pl.when(set_in(gives[w], 0))
        def _():
            hop(0, w, chip).start()


    q_column = column(q_gain[...])
    for i in range(4):
        load_q[i].wait()
        two = jnp.dot(normed[...], wq[i], preferred_element_type=F32)
        for u in range(2):
            h = 2 * i + u
            x = scaled_and_rotated(two[:, u * HEAD : (u + 1) * HEAD].T, q_column, sine, cosine)
            q_t[:HEAD, h * ROWS : (h + 1) * ROWS] = x.astype(BF16)

    ones = jnp.ones((16, ROWS), BF16)

    def keys_of(block):
        key_at = lax.broadcasted_iota(jnp.int32, (ROWS, HEAD), 0) + block * ROWS
        segment = jnp.where((key_at >= first_of) & (key_at < end_of), 1.0, 0.0).astype(BF16)
        return jnp.concatenate([kv[block, :, :HEAD], segment], axis=1)

    def values_of(block):
        values = jnp.concatenate([kv[block, :HEAD, HEAD:], kv[block, HEAD:, HEAD:]], axis=1)
        return jnp.concatenate([values, ones], axis=0)

    def scores(keys, turn, at, own=False):
        s = jnp.dot(keys, q_t[:, at], preferred_element_type=F32)
        if own:
            later = lax.broadcasted_iota(jnp.int32, s.shape, 0) > lax.broadcasted_iota(jnp.int32, s.shape, 1)
            s = jnp.where(later, masked_score, s)
        score[turn, :, at] = s
        peak[turn, :, at] = jnp.max(s.reshape(ROWS // 8, 8, -1), axis=0)

    def softmax(turn, at):
        before = top[:, at]
        highest = jnp.maximum(before, jnp.max(peak[turn, :, at], axis=0, keepdims=True) * score_scale_2)
        top[:, at] = highest
        factor[turn, :, at] = jnp.exp2(before - highest)
        weight[turn, :, at] = jnp.exp2(score[turn, :, at] * score_scale_2 - highest[:1]).astype(BF16)

    def mix(values, turn, at):
        mixed = jnp.dot(values, weight[turn, :, at], preferred_element_type=F32)
        state[:, at] = state[:, at] * factor[turn, :1, at] + mixed

    groups = [slice(at, at + WIDE) for at in range(0, 2048, WIDE)]

    state[...] = jnp.zeros_like(state)
    top[...] = jnp.full_like(top, masked_score)
    weight[1] = jnp.zeros_like(weight[1])
    factor[1] = jnp.ones_like(factor[1])
    own_keys = keys_of(chip)
    for h in range(8):
        scores(own_keys, 0, slice(h * ROWS, (h + 1) * ROWS), True)

    def compute(i, carry):
        count, last, second = carry
        block = block_at(looked_up(i))
        wanted = (block < chip) & (block >= chip - REACH)
        for turn in range(2):

            @pl.when(wanted & (lax.rem(count, 2) != turn))
            def _():
                keys, values = keys_of(block), values_of(second)
                for at in groups:
                    scores(keys, turn, at)
                    softmax(1 - turn, at)
                    mix(values, turn, at)

        return jnp.where(wanted, count + 1, count), jnp.where(wanted, block, last), jnp.where(wanted, last, second)

    def slot(t, carry):
        before = jnp.maximum(t - LAG, 0)
        for w in range(6):

            @pl.when(set_in(takes[w], before) & (t >= LAG))
            def _():
                hop(before, w, block_at(looked_up(before * 6 + w))).wait_recv()

        for w in range(6):

            @pl.when(set_in(gives[w], t))
            def _():
                hop(t, w, block_at(looked_up(t * 6 + w), ways[w])).start()

        first = before * 6
        return lax.fori_loop(first, jnp.where(t >= LAG, first + 6, first), compute, carry)

    count, last, second = lax.fori_loop(1, SLOTS + LAG, slot, (jnp.int32(0), chip, chip))
    for turn in range(2):

        @pl.when(lax.rem(count, 2) == turn)
        def _():
            before, now = values_of(second), values_of(last)
            for at in groups:
                softmax(turn, at)
                mix(before, 1 - turn, at)
                mix(now, turn, at)

    load_o.wait()
    for h in range(8):
        at = slice(h * ROWS, (h + 1) * ROWS)
        x = state[:HEAD, at] * (1.0 / state[HEAD : HEAD + 1, at])
        attended[:, h * HEAD : (h + 1) * HEAD] = x.T.astype(BF16)
    theirs = pl.ds(pl.multiple_of((1 - server) * HEAD, HEAD), HEAD)
    mine = pl.ds(pl.multiple_of(server * HEAD, HEAD), HEAD)
    swaps = []
    for n in range(4):
        at = slice(n * 512, (n + 1) * 512)
        sent[n] = jnp.dot(attended[theirs, :], wo[:, at], preferred_element_type=F32).astype(BF16)
        swap = pltpu.make_async_remote_copy(
            src_ref=sent.at[n],
            dst_ref=received.at[n],
            send_sem=swap_sem.at[0, n],
            recv_sem=swap_sem.at[1, n],
            device_id={"srv": 1 - server},
            device_id_type=MESH,
        )
        swap.start()
        swaps.append(swap)
    for n in range(4):
        at = slice(n * 512, (n + 1) * 512)
        part = jnp.dot(attended[mine, :], wo[:, at], preferred_element_type=F32)
        swaps[n].wait_recv()
        out[:, at] = (part + received[n].astype(F32)).astype(BF16)
    for n in range(4):
        swaps[n].wait_send()

    def left(t, carry):
        for w in range(6):

            @pl.when(set_in(gives[w], t))
            def _():
                hop(t, w, chip).wait_send()

        return carry

    lax.fori_loop(0, SLOTS, left, 0)


def local(
    tokens, norm_gain, q_gain, k_gain, w_query, w_key, w_value, w_out, doc_lengths, stretch_offsets
):
    half = jnp.arange(HEAD // 2, dtype=F32)
    frequency = rope_base ** (-2.0 * jnp.concatenate([half, half]) / HEAD)
    vmem = pl.BlockSpec(memory_space=pltpu.VMEM)
    smem = pl.BlockSpec(memory_space=pltpu.SMEM)
    hbm = pl.BlockSpec(memory_space=pl.ANY)
    dma = pltpu.SemaphoreType.DMA
    return pl.pallas_call(
        kernel,
        out_shape=jax.ShapeDtypeStruct((HEAD, 2048), BF16),
        in_specs=[hbm, vmem, vmem, vmem, vmem, hbm, hbm, hbm, hbm, smem, smem],
        out_specs=vmem,
        scratch_shapes=[
            pltpu.VMEM((ROWS, 2048), BF16),
            pltpu.VMEM((ROWS, 2048), BF16),
            pltpu.VMEM((2048, 256), BF16),
            pltpu.VMEM((4, 2048, 256), BF16),
            pltpu.VMEM((1024, 2048), BF16),
            pltpu.VMEM((BLOCKS, ROWS, 256), BF16),
            pltpu.VMEM((256, 2048), BF16),
            pltpu.VMEM((2, ROWS, 2048), F32),
            pltpu.VMEM((2, 8, 2048), F32),
            pltpu.VMEM((2, ROWS, 2048), BF16),
            pltpu.VMEM((2, 8, 2048), F32),
            pltpu.VMEM((HEAD + 16, 2048), F32),
            pltpu.VMEM((8, 2048), F32),
            pltpu.VMEM((ROWS, 1024), BF16),
            pltpu.VMEM((4, HEAD, 512), BF16),
            pltpu.VMEM((4, HEAD, 512), BF16),
            dma((4,)),
            dma((4,)),
            dma((SLOTS * 6,)),
            dma((SLOTS * 6,)),
            dma((2, 4)),
        ],
        compiler_params=pltpu.CompilerParams(
            collective_id=0, has_side_effects=True, vmem_limit_bytes=60 * 2**20
        ),
        name="attention_layer",
    )(
        tokens,
        norm_gain.reshape(1, -1),
        q_gain.reshape(1, -1),
        k_gain.reshape(1, -1),
        frequency.reshape(1, -1),
        w_query,
        w_key,
        w_value,
        w_out,
        doc_lengths,
        stretch_offsets,
    )


def solution(mesh):
    return jax.shard_map(
        local,
        mesh=mesh,
        in_specs=(
            P("ctx", None),
            P(),
            P(),
            P(),
            P(None, "srv"),
            P(),
            P(),
            P("srv", None),
            P(),
            P("ctx"),
        ),
        out_specs=P(("ctx", "srv"), None),
        check_vma=False,
    )
```
